256 devices in a mesh: section: 2 (over x_hi), expert: 64 (over z, y, x_lo), dp: 2 (over core).
Axes of the slice: x: 4 (x_hi: 2, x_lo: 2; x = x_hi * 2 + x_lo), y: 4, z: 8, core: 2. Of those that a mesh axis runs over, the one named last changes fastest.
Arguments:
- tokens: bfloat16 [2, 16384, 3072], P('section', ('expert', 'dp')), may hold values from -6 to 6
- expert_ids: int32 [2, 16384, 2], P('section', ('expert', 'dp')), may hold values from 0 to 63, all different within a row; in each aligned block of 64 rows (0 to 63, 64 to 127, ..., all dimensions but the last counted through in order) at most 4 rows name the same one
- combine: bfloat16 [2, 16384, 2], P('section', ('expert', 'dp')), may hold values from 0.099609375 to 0.8984375
- upstream: bfloat16 [2, 16384, 3072], P('section', ('expert', 'dp')), may hold values from -6 to 6
- w_gate: bfloat16 [2, 64, 3072, 128], P('section', 'expert', 'dp'), may hold values from -0.109375 to 0.109375
- w_up: bfloat16 [2, 64, 3072, 128], P('section', 'expert', 'dp'), may hold values from -0.109375 to 0.109375
- w_down: bfloat16 [2, 64, 128, 3072], P('section', 'expert', None, 'dp'), may hold values from -0.5 to 0.5
Outputs:
- grad_x: bfloat16 [2, 16384, 3072], P('section', ('expert', 'dp'))
- grad_combine: bfloat16 [2, 16384, 2], P('section', ('expert', 'dp'))
- grad_gate: bfloat16 [2, 64, 3072, 128], P('section', 'expert', 'dp')
- grad_up: bfloat16 [2, 64, 3072, 128], P('section', 'expert', 'dp')
- grad_down: bfloat16 [2, 64, 128, 3072], P('section', 'expert', None, 'dp')
The draws below stay inside these ranges and needn't reach their ends.
Inputs may be any that keep to these rules, and one draw needn't show every extreme that they name: `expert_ids`: each token names two different experts. In each aligned block of 64 tokens (one micro-batch of one device) no expert is named by more than 4 tokens, and this bound is reached in some block.
All inputs are finite; a program needn't handle non-finite values.
Results may differ from the reference program's by a relative error of at most 0.0065.
Values may be sent and summed in bfloat16 or wider, within the bound.
No kernel may reach another device: no remote copies, remote signals or barrier semaphores. Data moves between devices by JAX's collectives and lax.ppermute only.
A program may use at most 64 MiB of HBM per device.

```python
import math
import jax
import jax.numpy as jnp
import numpy as np
from jax import lax

D = 3072
FF = 128
MICRO = 2
TOK_MB = 64
CAP = 4
EXPERTS = 64
TOKENS = 16384
N_SECTION = 2
N_EXPERT = 64
N_DP = 2


def level_of(stream_key, extent, split, low, top_value):
    def one(dim, parts):
        heights = jax.random.uniform(jax.random.fold_in(jax.random.fold_in(stream_key, 6), dim), (parts,), jnp.float32, low / len(split), top_value / len(split))
        return jnp.repeat(jnp.exp(heights), extent[dim] // parts).reshape((-1,) + (1,) * (len(extent) - dim - 1))

    level = one(*split[0])
    for cut in split[1:]:
        level = level * one(*cut)
    return level


def routed_block(rng, own, number, rows, number_of, top, reach, skew):
    order = jax.random.permutation(rng, number_of)
    packed, usual = shares(number_of, rows * top, reach, skew, True), shares(number_of, rows * top, reach, skew, False)
    places = jnp.arange(number_of)

    def named(tallies, turn):
        used = int((tallies > 0).sum())
        fixed = max(1, used // 4)
        moved = fixed + (places - fixed + turn * (used - fixed)) % max(1, number_of - fixed)
        return jnp.zeros((number_of,), jnp.int32).at[order[jnp.where(places < fixed, places, moved)]].set(jnp.asarray(tallies, jnp.int32))

    tallies = jnp.where(number % 4 == 0, named(packed, number // 4), named(usual, number - number // 4 - 1))
    mixed = jax.random.permutation(jax.random.fold_in(own, 3), number_of)
    source_of, taker = mixed[0:number_of // 2 * 2:2], mixed[1:number_of // 2 * 2:2]
    margin = jnp.minimum(tallies[source_of] - 1, reach - tallies[taker]) // 2
    margin = jnp.where((source_of == order[0]) | (taker == order[0]) | (tallies[taker] == 0), 0, jnp.maximum(margin, 0))
    moved = jax.random.randint(jax.random.fold_in(own, 4), (number_of // 2,), 0, 1 << 20) % (margin + 1)
    tallies = tallies.at[source_of].add(-moved).at[taker].add(moved)
    members = jnp.searchsorted(jnp.cumsum(tallies), jnp.arange(rows * top), side="right").astype(jnp.int32)
    grid = members.reshape(top, rows).T
    grid = grid[jax.random.permutation(jax.random.fold_in(own, 1), rows)]
    turn = jax.random.randint(jax.random.fold_in(own, 2), (rows, 1), 0, top)
    return jnp.take_along_axis(grid, (jnp.arange(top)[None, :] + turn) % top, axis=1)


def shares(amount, total, most, slope, full):
    portions = [(1 << 20) // math.isqrt(grade ** slope) + 1 for grade in range(1, amount + 1)]
    largest = most if full else min(most, max(-(-total // amount), total * portions[0] // sum(portions)))
    least = 1 if total - largest >= amount - 1 else 0
    given, spare = [largest] + [least] * (amount - 1), total - largest - least * (amount - 1)
    while spare > 0:
        free = [i for i in range(1, amount) if given[i] < largest] or [i for i in range(1, amount) if given[i] < most]
        whole, left = sum([portions[i] for i in free]), spare
        for i in free:
            addition = min(most - given[i], max(1, left * portions[i] // whole), spare)
            given[i] = given[i] + addition
            spare = spare - addition
    return np.array(given)


def bell_draw(rng, extent, width, reach, pieces=(), kind=jnp.bfloat16):
    entries = jax.random.normal(rng, extent, jnp.float32) * width
    if len(pieces) > 0:
        entries = level_of(rng, extent, pieces, -0.22, 0.18) * entries
    return jnp.clip(entries, min=-reach, max=reach).astype(kind)


def setup_inputs(seed: int = 0) -> dict:
    seeds = jax.random.split(jax.random.key(seed), 8)
    tokens = bell_draw(seeds[0], (N_SECTION, TOKENS, D), 1.0, 6.0, ((0, 2), (1, 128)))
    expert_ids_keys = jax.random.split(jax.random.fold_in(seeds[1], 1), N_SECTION * TOKENS // TOK_MB)
    expert_ids_turns = jax.random.permutation(jax.random.fold_in(seeds[1], 3), N_SECTION * TOKENS // TOK_MB)
    expert_ids = jax.vmap(lambda own, number: routed_block(jax.random.fold_in(seeds[1], 2), own, number, TOK_MB, EXPERTS, 2, CAP, 2))(expert_ids_keys, expert_ids_turns).reshape((N_SECTION, TOKENS, 2))
    combine = jnp.clip(0.099609375 + 0.7988281 * jax.random.uniform(seeds[2], (N_SECTION, TOKENS, 2), jnp.float32) ** level_of(seeds[2], (N_SECTION, TOKENS, 2), ((0, 2), (1, 128)), -0.2, 0.2), 0.099609375, 0.8984375).astype(jnp.bfloat16)
    upstream = bell_draw(seeds[3], (N_SECTION, TOKENS, D), 1.0, 6.0, ((0, 2), (1, 128)))
    w_gate = bell_draw(seeds[4], (N_SECTION, EXPERTS, D, FF), D ** -0.5, 0.109375, ((0, 2), (1, 64), (2, 2)))
    w_up = bell_draw(seeds[5], (N_SECTION, EXPERTS, D, FF), D ** -0.5, 0.109375, ((0, 2), (1, 64), (2, 2)))
    w_down = bell_draw(seeds[6], (N_SECTION, EXPERTS, FF, D), FF ** -0.5, 0.5, ((0, 2), (1, 64), (3, 2)))
    return dict(tokens=tokens, expert_ids=expert_ids, combine=combine, upstream=upstream, w_gate=w_gate, w_up=w_up, w_down=w_down)


def slot_table(block_ids):
    flat_ids = block_ids.reshape(-1)
    labels = jnp.arange(EXPERTS, dtype=jnp.int32)
    hits_mask = (flat_ids[:, None] == labels[None, :]).astype(jnp.int32)
    earlier = jnp.cumsum(hits_mask, axis=0) - hits_mask
    position = jnp.sum(earlier * hits_mask, axis=1)
    target = flat_ids * CAP + position
    columns = jnp.arange(EXPERTS * CAP, dtype=jnp.int32)
    picked = (target[:, None] == columns[None, :]).astype(jnp.float32)
    return picked.reshape(TOK_MB, 2, EXPERTS * CAP)


def regroup(array):
    tail = array.shape[3:]
    array = array.reshape((N_EXPERT, MICRO, EXPERTS, CAP) + tail)
    array = jnp.moveaxis(array, 2, 0)
    return array.reshape((EXPERTS, N_EXPERT * MICRO * CAP) + tail)


def ungroup(array):
    tail = array.shape[2:]
    array = array.reshape((EXPERTS, N_EXPERT, MICRO, CAP) + tail)
    array = jnp.moveaxis(array, 0, 2)
    return array.reshape((N_EXPERT, MICRO, EXPERTS * CAP) + tail)


def group_pass(tokens_segment, ids_segment, combine_segment, upstream_segment, gate_segment, up_segment, down_segment, group_index):
    layout = (N_EXPERT, N_DP, MICRO, TOK_MB)
    token_rows = jnp.take(tokens_segment.reshape(layout + (D,)), group_index, axis=1)
    token_ids = jnp.take(ids_segment.reshape(layout + (2,)), group_index, axis=1)
    token_comb = jnp.take(combine_segment.reshape(layout + (2,)), group_index, axis=1)
    token_up = jnp.take(upstream_segment.reshape(layout + (D,)), group_index, axis=1)
    picked = jax.vmap(jax.vmap(slot_table))(token_ids)
    token_table = jnp.sum(picked, axis=3)
    rows_half = jnp.einsum("imtc,imtd->imcd", token_table, token_rows.astype(jnp.float32)).astype(jnp.bfloat16)
    grads_half = jnp.einsum("imtc,imtd->imcd", token_table, token_up.astype(jnp.float32)).astype(jnp.bfloat16)
    weight_half = jnp.einsum("imtkc,imtk->imc", picked, token_comb.astype(jnp.float32)).astype(jnp.bfloat16)
    rows_wide = regroup(rows_half).astype(jnp.float32)
    grads_wide = regroup(grads_half).astype(jnp.float32)
    weight_wide = regroup(weight_half).astype(jnp.float32)
    gate_wide = gate_segment.astype(jnp.float32)
    up_wide = up_segment.astype(jnp.float32)
    down_wide = down_segment.astype(jnp.float32)
    gate_pre = jnp.einsum("erd,edf->erf", rows_wide, gate_wide)
    up_pre = jnp.einsum("erd,edf->erf", rows_wide, up_wide)
    sigmoid_gate = jax.nn.sigmoid(gate_pre)
    active = gate_pre * sigmoid_gate
    hidden = (active * up_pre).astype(jnp.bfloat16)
    hidden_wide = hidden.astype(jnp.float32)
    expert_out = jnp.einsum("erf,efd->erd", hidden_wide, down_wide)
    weight_grad = jnp.sum(expert_out * grads_wide, axis=2).astype(jnp.bfloat16)
    scaled = (weight_wide[:, :, None] * grads_wide).astype(jnp.bfloat16)
    scaled_wide = scaled.astype(jnp.float32)
    hidden_grad = jnp.einsum("erd,efd->erf", scaled_wide, down_wide)
    gate_grad = (hidden_grad * up_pre * sigmoid_gate * (1.0 + gate_pre * (1.0 - sigmoid_gate))).astype(jnp.bfloat16)
    up_grad = (hidden_grad * active).astype(jnp.bfloat16)
    gate_grad_wide = gate_grad.astype(jnp.float32)
    up_grad_wide = up_grad.astype(jnp.float32)
    back_rows = (jnp.einsum("erf,edf->erd", gate_grad_wide, gate_wide) + jnp.einsum("erf,edf->erd", up_grad_wide, up_wide)).astype(jnp.bfloat16)
    back_tokens = ungroup(back_rows).astype(jnp.float32)
    token_grad = jnp.einsum("imtc,imcd->imtd", token_table, back_tokens).astype(jnp.bfloat16)
    back_weight = ungroup(weight_grad).astype(jnp.float32)
    weight_out = jnp.einsum("imtkc,imc->imtk", picked, back_weight).astype(jnp.bfloat16)
    part_gate = jnp.einsum("erd,erf->edf", rows_wide, gate_grad_wide).astype(jnp.bfloat16)
    part_up = jnp.einsum("erd,erf->edf", rows_wide, up_grad_wide).astype(jnp.bfloat16)
    part_down = jnp.einsum("erf,erd->efd", hidden_wide, scaled_wide).astype(jnp.bfloat16)
    return token_grad, weight_out, part_gate, part_up, part_down


def reference(tokens, expert_ids, combine, upstream, w_gate, w_up, w_down):
    grads_list = []
    comb_list = []
    gate_list = []
    up_list = []
    down_list = []
    for segment_index in range(N_SECTION):
        def one_group(group_index):
            return group_pass(tokens[segment_index], expert_ids[segment_index], combine[segment_index], upstream[segment_index], w_gate[segment_index], w_up[segment_index], w_down[segment_index], group_index)

        token_grad, weight_out, part_gate, part_up, part_down = lax.map(one_group, jnp.arange(N_DP, dtype=jnp.int32))
        grads_list.append(jnp.swapaxes(token_grad, 0, 1).reshape(TOKENS, D))
        comb_list.append(jnp.swapaxes(weight_out, 0, 1).reshape(TOKENS, 2))
        gate_list.append(jnp.sum(part_gate.astype(jnp.float32), axis=0).astype(jnp.bfloat16))
        up_list.append(jnp.sum(part_up.astype(jnp.float32), axis=0).astype(jnp.bfloat16))
        down_list.append(jnp.sum(part_down.astype(jnp.float32), axis=0).astype(jnp.bfloat16))
    grad_x = jnp.roll(jnp.stack(grads_list), -1, axis=0)
    return (grad_x, jnp.stack(comb_list), jnp.stack(gate_list), jnp.stack(up_list), jnp.stack(down_list))
```

```python
import functools

import jax
import jax.numpy as jnp
from jax import lax
from jax.experimental import pallas as pl
from jax.experimental.pallas import tpu as pltpu
from jax.sharding import PartitionSpec as P

TOK_MB = 64
CAP = 4
LANES = 128
VMEM_LIMIT = 48 * 1024 * 1024


def contract_rows(former, latter):
    return lax.dot_general(
        former, latter, (((0,), (0,)), ((), ())), preferred_element_type=jnp.float32
    )


def dispatch_kernel(slots, x_steps, ids_ref, comb_ref, tok_ref, up_ref, out_ref, pick_ref, plain, scaled):
    step = pl.program_id(0)
    rows = ids_ref.shape[0]
    per_expert = slots * CAP

    @pl.when(step == 0)
    def _():
        ids = ids_ref[...]
        first, second = ids[:, 0:1], ids[:, 1:2]
        label = lax.broadcasted_iota(jnp.int32, (rows, LANES), 1)
        hit0 = (first == label).astype(jnp.float32)
        hit1 = (second == label).astype(jnp.float32)
        row = lax.broadcasted_iota(jnp.int32, (rows, rows), 0)
        col = lax.broadcasted_iota(jnp.int32, (rows, rows), 1)
        before = ((col < row) & (col // TOK_MB == row // TOK_MB)).astype(jnp.bfloat16)
        earlier = jnp.dot(
            before, (hit0 + hit1).astype(jnp.bfloat16), preferred_element_type=jnp.float32
        )
        place0 = jnp.sum(earlier * hit0, axis=1, keepdims=True).astype(jnp.int32)
        place1 = jnp.sum(earlier * hit1, axis=1, keepdims=True).astype(jnp.int32)
        block = lax.broadcasted_iota(jnp.int32, (rows, 1), 0) // TOK_MB
        width = pick_ref.shape[1]
        column = lax.broadcasted_iota(jnp.int32, (rows, width), 1)
        table0 = (first * per_expert + block * CAP + place0 == column).astype(jnp.float32)
        table1 = (second * per_expert + block * CAP + place1 == column).astype(jnp.float32)
        comb = comb_ref[...].astype(jnp.float32)
        plain[...] = (table0 + table1).astype(jnp.bfloat16)
        scaled[...] = (table0 * comb[:, 0:1] + table1 * comb[:, 1:2]).astype(jnp.bfloat16)
        pick_ref[0:rows, :] = table0.astype(jnp.bfloat16)
        pick_ref[rows : 2 * rows, :] = table1.astype(jnp.bfloat16)

    @pl.when(step < x_steps)
    def _():
        out_ref[...] = contract_rows(plain[...], tok_ref[...]).astype(jnp.bfloat16)

    @pl.when(step >= x_steps)
    def _():
        out_ref[...] = contract_rows(scaled[...], up_ref[...]).astype(jnp.bfloat16)


def dispatch(ids, comb, tok, up, expert_count):
    rows, width = tok.shape
    slots = rows // TOK_MB
    total = expert_count * slots * CAP
    tile = 1024
    steps = width // tile
    return pl.pallas_call(
        functools.partial(dispatch_kernel, slots, steps),
        grid=(2 * steps,),
        in_specs=[
            pl.BlockSpec((rows, 2), lambda i: (0, 0)),
            pl.BlockSpec((rows, 2), lambda i: (0, 0)),
            pl.BlockSpec((rows, tile), lambda i: (0, jnp.minimum(i, steps - 1))),
            pl.BlockSpec((rows, tile), lambda i: (0, jnp.maximum(i - steps, 0))),
        ],
        out_specs=[
            pl.BlockSpec((total, tile), lambda i: (0, i)),
            pl.BlockSpec((2 * rows, total), lambda i: (0, 0)),
        ],
        out_shape=[
            jax.ShapeDtypeStruct((total, 2 * width), jnp.bfloat16),
            jax.ShapeDtypeStruct((2 * rows, total), jnp.bfloat16),
        ],
        scratch_shapes=[
            pltpu.VMEM((rows, total), jnp.bfloat16),
            pltpu.VMEM((rows, total), jnp.bfloat16),
        ],
        compiler_params=pltpu.CompilerParams(vmem_limit_bytes=VMEM_LIMIT),
        name="dispatch_rows",
    )(ids, comb, tok, up)


def expert_kernel(cut, row_ref, wgu_ref, wgu_t_ref, wd_t_ref, out0_ref, out1_ref, act_ref):
    width = wgu_ref.shape[0]
    hid = wd_t_ref.shape[1]
    pre = jnp.dot(row_ref[:, :width], wgu_ref[...], preferred_element_type=jnp.float32)
    hidden_grad = jnp.dot(row_ref[:, width:], wd_t_ref[...], preferred_element_type=jnp.float32)
    gate_pre, up_pre = pre[:, :hid], pre[:, hid:]
    sig = jax.nn.sigmoid(gate_pre)
    active = gate_pre * sig
    hidden = (active * up_pre).astype(jnp.bfloat16)
    gate_grad = (hidden_grad * up_pre * sig * (1.0 + gate_pre * (1.0 - sig))).astype(jnp.bfloat16)
    up_grad = (hidden_grad * active).astype(jnp.bfloat16)
    both = jnp.concatenate([gate_grad, up_grad], axis=1)
    act_ref[:, :hid] = hidden
    act_ref[:, hid:] = both
    weight = jnp.sum(hidden.astype(jnp.float32) * hidden_grad, axis=1, keepdims=True)
    out0_ref[...] = jnp.dot(
        both, wgu_t_ref[:, :cut], preferred_element_type=jnp.float32
    ).astype(jnp.bfloat16)
    out1_ref[:, : width - cut] = jnp.dot(
        both, wgu_t_ref[:, cut:], preferred_element_type=jnp.float32
    ).astype(jnp.bfloat16)
    out1_ref[:, width - cut :] = jnp.broadcast_to(weight, (weight.shape[0], LANES)).astype(
        jnp.bfloat16
    )


def expert_pass(rows, wgu, wgu_t, wd_t, cut):
    count = rows.shape[0]
    width, pair = wgu.shape
    hid = wd_t.shape[1]
    tile = 128
    return pl.pallas_call(
        functools.partial(expert_kernel, cut),
        grid=(count // tile,),
        in_specs=[
            pl.BlockSpec((tile, 2 * width), lambda i: (i, 0)),
            pl.BlockSpec((width, pair), lambda i: (0, 0)),
            pl.BlockSpec((pair, width), lambda i: (0, 0)),
            pl.BlockSpec((width, hid), lambda i: (0, 0)),
        ],
        out_specs=[
            pl.BlockSpec((tile, cut), lambda i: (i, 0)),
            pl.BlockSpec((tile, width - cut + LANES), lambda i: (i, 0)),
            pl.BlockSpec((tile, hid + pair), lambda i: (i, 0)),
        ],
        out_shape=[
            jax.ShapeDtypeStruct((count, cut), jnp.bfloat16),
            jax.ShapeDtypeStruct((count, width - cut + LANES), jnp.bfloat16),
            jax.ShapeDtypeStruct((count, hid + pair), jnp.bfloat16),
        ],
        compiler_params=pltpu.CompilerParams(vmem_limit_bytes=VMEM_LIMIT),
        name="expert_rows",
    )(rows, wgu, wgu_t, wd_t)


def exchanged(array, axis_name):
    return lax.all_to_all(array, axis_name, split_axis=0, concat_axis=0, tiled=True)


def summed_over_dp(part, dim):
    half = part.shape[dim] // 2
    me = lax.axis_index("dp")
    mine = lax.dynamic_slice_in_dim(part, me * half, half, dim)
    other = lax.dynamic_slice_in_dim(part, (1 - me) * half, half, dim)
    came = lax.ppermute(other, "dp", [(0, 1), (1, 0)])
    return (mine.astype(jnp.float32) + came.astype(jnp.float32)).astype(jnp.bfloat16)


def body(tokens, expert_ids, combine, upstream, w_gate, w_up, w_down):
    expert_count = lax.axis_size("expert")
    sections = lax.axis_size("section")
    width = tokens.shape[2]
    rows = tokens.shape[1]
    per_expert = rows // TOK_MB * CAP
    cut = width * 3 // 4
    back_by_one = [(i, (i - 1) % sections) for i in range(sections)]

    send, pick = dispatch(expert_ids[0], combine[0], tokens[0], upstream[0], expert_count)
    came = exchanged(send.reshape(expert_count, per_expert, 2 * width), "expert")
    came = came.reshape(expert_count * per_expert, 2 * width)

    gate_full = lax.all_gather(w_gate[0, 0], "dp", axis=0, tiled=True)
    up_full = lax.all_gather(w_up[0, 0], "dp", axis=0, tiled=True)
    down_full = lax.all_gather(w_down[0, 0], "dp", axis=1, tiled=True)
    wgu = jnp.concatenate([gate_full, up_full], axis=1)
    wgu_t = wgu.T
    wd_t = down_full.T

    out0, out1, acts = expert_pass(came, wgu, wgu_t, wd_t, cut)
    hid = wd_t.shape[1]

    back0 = exchanged(out0.reshape(expert_count, per_expert, cut), "expert")
    out1 = out1.reshape(expert_count, per_expert, width - cut + LANES)
    out1, back0 = lax.optimization_barrier((out1, back0))
    back1 = exchanged(out1, "expert")

    both_picks = pick[:rows] + pick[rows:]
    grad0 = jnp.dot(
        both_picks, back0.reshape(-1, cut), preferred_element_type=jnp.float32
    ).astype(jnp.bfloat16)
    grad0 = lax.ppermute(grad0, "section", back_by_one)
    tail = jnp.dot(
        pick, back1.reshape(-1, width - cut + LANES), preferred_element_type=jnp.float32
    )
    grad1 = (tail[:rows, : width - cut] + tail[rows:, : width - cut]).astype(jnp.bfloat16)
    grad1 = lax.ppermute(grad1, "section", back_by_one)
    weight = jnp.stack([tail[:rows, width - cut], tail[rows:, width - cut]], axis=1)
    grad_combine = (weight / combine[0].astype(jnp.float32)).astype(jnp.bfloat16)

    part_gu = contract_rows(came[:, :width], acts[:, hid:]).astype(jnp.bfloat16)
    part_down = contract_rows(acts[:, :hid], came[:, width:]).astype(jnp.bfloat16)
    grad_gu = summed_over_dp(part_gu, 0)
    grad_down = summed_over_dp(part_down, 1)
    return (
        jnp.concatenate([grad0, grad1], axis=1)[None],
        grad_combine[None],
        grad_gu[:, :hid][None, None],
        grad_gu[:, hid:][None, None],
        grad_down[None, None],
    )


def solution(mesh):
    return jax.shard_map(
        body,
        mesh=mesh,
        in_specs=(
            P("section", ("expert", "dp"), None),
            P("section", ("expert", "dp"), None),
            P("section", ("expert", "dp"), None),
            P("section", ("expert", "dp"), None),
            P("section", "expert", "dp", None),
            P("section", "expert", "dp", None),
            P("section", "expert", None, "dp"),
        ),
        out_specs=(
            P("section", ("expert", "dp"), None),
            P("section", ("expert", "dp"), None),
            P("section", "expert", "dp", None),
            P("section", "expert", "dp", None),
            P("section", "expert", None, "dp"),
        ),
        check_vma=False,
    )
```

```python
import functools

import jax
import jax.numpy as jnp
from jax import lax
from jax.experimental import pallas as pl
from jax.experimental.pallas import tpu as pltpu
from jax.sharding import PartitionSpec as P

TOK_MB = 64
CAP = 4
LANES = 128
PLANES = 8
EXPERTS_PLANE = 8
IN_PLANE = [[z * EXPERTS_PLANE + c for c in range(EXPERTS_PLANE)] for z in range(PLANES)]
CHUNKS = ((0,), (1, -1), (2, -2), (3, -3), (4,))
RETURNS = ((0,), (1, -1, 2, -2), (3, -3, 4))
VMEM_LIMIT = 48 * 1024 * 1024
COST = 60000000000


def contract_rows(former, latter):
    return lax.dot_general(
        former, latter, (((0,), (0,)), ((), ())), preferred_element_type=jnp.float32
    )


def plane_tables(meta, plane, source_count, position):
    columns = EXPERTS_PLANE
    meta = meta.astype(jnp.float32).T
    rows = meta.shape[1]
    first, second = meta[0:1, :].astype(jnp.int32), meta[1:2, :].astype(jnp.int32)
    label = lax.broadcasted_iota(jnp.int32, (columns, rows), 0) + plane * columns
    hit0 = (first == label).astype(jnp.float32)
    hit1 = (second == label).astype(jnp.float32)
    row = lax.broadcasted_iota(jnp.int32, (rows, rows), 0)
    col = lax.broadcasted_iota(jnp.int32, (rows, rows), 1)
    before = ((row < col) & (row // TOK_MB == col // TOK_MB)).astype(jnp.bfloat16)
    earlier = jnp.dot(
        (hit0 + hit1).astype(jnp.bfloat16), before, preferred_element_type=jnp.float32
    )
    per_expert = rows // TOK_MB * CAP
    spot = lax.broadcasted_iota(jnp.int32, (1, rows), 1) // TOK_MB * CAP + position * per_expert
    total = columns * per_expert * source_count
    slot = lax.broadcasted_iota(jnp.int32, (total, rows), 0)

    def table(chosen, hit):
        place = jnp.sum(earlier * hit, axis=0, keepdims=True).astype(jnp.int32)
        column = chosen - plane * columns
        inside = (column >= 0) & (column < columns)
        target = jnp.where(inside, column * (per_expert * source_count) + spot + place, -1)
        return (slot == target).astype(jnp.float32)

    table0, table1 = table(first, hit0), table(second, hit1)
    plain = (table0 + table1).astype(jnp.bfloat16)
    scaled = (table0 * meta[2:3, :] + table1 * meta[3:4, :]).astype(jnp.bfloat16)
    return plain, scaled


def plane_kernel(count, x_steps, z_ref, *refs):
    mark_refs, row_refs = refs[:count], refs[count : 2 * count]
    out_ref, table = refs[2 * count :]
    step = pl.program_id(0)

    @pl.when(step == 0)
    def _():
        for place in range(count):
            plain, scaled = plane_tables(mark_refs[place][...], z_ref[0], count, place)
            table[2 * place] = plain
            table[2 * place + 1] = scaled

    kind = (step >= x_steps).astype(jnp.int32)
    total = None
    for place in range(count):
        part = jnp.dot(
            table[2 * place + kind], row_refs[place][...], preferred_element_type=jnp.float32
        )
        total = part if total is None else total + part
    out_ref[...] = total.astype(jnp.bfloat16)


def plane_rows(z, sources):
    rows, full = sources[0].shape
    count = len(sources)
    width = (full - LANES) // 2
    total = EXPERTS_PLANE * rows // TOK_MB * CAP * count
    tile = width // 2
    steps = width // tile
    return pl.pallas_call(
        functools.partial(plane_kernel, count, steps),
        grid=(2 * steps,),
        in_specs=[pl.BlockSpec(memory_space=pltpu.SMEM)]
        + [pl.BlockSpec((rows, LANES), lambda i: (0, 2 * width // LANES))] * count
        + [pl.BlockSpec((rows, tile), lambda i: (0, i))] * count,
        out_specs=pl.BlockSpec((total, tile), lambda i: (0, i)),
        out_shape=jax.ShapeDtypeStruct((total, 2 * width), jnp.bfloat16),
        scratch_shapes=[pltpu.VMEM((2 * count, total, rows), jnp.bfloat16)],
        compiler_params=pltpu.CompilerParams(vmem_limit_bytes=VMEM_LIMIT),
        name="plane_rows",
    )(z, *sources, *sources)


def onward_kernel(steps, z_ref, mark_a, mark_b, row_a, row_b, near_a, near_b, far_a, far_b, table):
    step = pl.program_id(0)
    slots = near_a.shape[0]

    @pl.when(step == 0)
    def _():
        for way, (mark_ref, sign) in enumerate(((mark_a, 1), (mark_b, -1))):
            for hop in (0, 1):
                plane = lax.rem(z_ref[0] + (PLANES + (hop + 1) * sign), PLANES)
                plain, scaled = plane_tables(mark_ref[...], plane, 1, 0)
                table[2 * way, hop * slots : (hop + 1) * slots, :] = plain
                table[2 * way + 1, hop * slots : (hop + 1) * slots, :] = scaled

    def product(table, side):
        return jnp.dot(table, side[...], preferred_element_type=jnp.float32).astype(jnp.bfloat16)

    @pl.when(step < steps)
    def _():
        both = product(table[0], row_a)
        near_a[...] = both[:slots]
        far_a[...] = both[slots:]
        near_b[...] = product(table[2, :slots, :], row_b)

    @pl.when(step >= steps)
    def _():
        near_a[...] = product(table[1, :slots, :], row_a)
        both = product(table[3], row_b)
        near_b[...] = both[:slots]
        far_b[...] = both[slots:]


def onward_rows(z, source_a, source_b):
    rows, full = source_a.shape
    width = (full - LANES) // 2
    total = EXPERTS_PLANE * rows // TOK_MB * CAP
    tile = width // 2
    steps = width // tile
    marks = pl.BlockSpec((rows, LANES), lambda i: (0, 2 * width // LANES))
    block = pl.BlockSpec((rows, tile), lambda i: (0, i))
    return pl.pallas_call(
        functools.partial(onward_kernel, steps),
        grid=(2 * steps,),
        in_specs=[pl.BlockSpec(memory_space=pltpu.SMEM), marks, marks, block, block],
        out_specs=[
            pl.BlockSpec((total, tile), lambda i: (0, i)),
            pl.BlockSpec((total, tile), lambda i: (0, i)),
            pl.BlockSpec((total, tile), lambda i: (0, jnp.minimum(i, steps - 1))),
            pl.BlockSpec((total, tile), lambda i: (0, jnp.maximum(i - steps, 0))),
        ],
        out_shape=[jax.ShapeDtypeStruct((total, 2 * width), jnp.bfloat16)] * 2
        + [jax.ShapeDtypeStruct((total, width), jnp.bfloat16)] * 2,
        scratch_shapes=[pltpu.VMEM((4, 2 * total, rows), jnp.bfloat16)],
        compiler_params=pltpu.CompilerParams(vmem_limit_bytes=VMEM_LIMIT),
        name="onward_rows",
    )(z, source_a, source_b, source_a, source_b)


def own_kernel(z_ref, ids_ref, *pick_refs):
    rows = ids_ref.shape[0]
    per_expert = rows // TOK_MB * CAP
    ids = ids_ref[...]
    label = lax.broadcasted_iota(jnp.int32, (rows, LANES), 1)
    hits = [(ids[:, k : k + 1] == label).astype(jnp.float32) for k in (0, 1)]
    row = lax.broadcasted_iota(jnp.int32, (rows, rows), 0)
    col = lax.broadcasted_iota(jnp.int32, (rows, rows), 1)
    before = ((col < row) & (col // TOK_MB == row // TOK_MB)).astype(jnp.bfloat16)
    earlier = jnp.dot(
        before, (hits[0] + hits[1]).astype(jnp.bfloat16), preferred_element_type=jnp.float32
    )
    block = lax.broadcasted_iota(jnp.int32, (rows, 1), 0) // TOK_MB
    for k in (0, 1):
        chosen = ids[:, k : k + 1]
        place = jnp.sum(earlier * hits[k], axis=1, keepdims=True).astype(jnp.int32)
        behind = (z_ref[0] - chosen // EXPERTS_PLANE + PLANES) % PLANES
        column = chosen % EXPERTS_PLANE
        for pick_ref, offsets in zip(pick_refs, RETURNS):
            spot = jnp.full((rows, 1), -1, jnp.int32)
            for turn, offset in enumerate(offsets):
                target = (column * len(offsets) + turn) * per_expert + block * CAP + place
                spot = jnp.where(behind == offset % PLANES, target, spot)
            slot = lax.broadcasted_iota(jnp.int32, (rows, pick_ref.shape[1]), 1)
            pick_ref[k * rows : (k + 1) * rows, :] = (slot == spot).astype(jnp.bfloat16)


def own_picks(z, ids):
    rows = ids.shape[0]
    group = EXPERTS_PLANE * rows // TOK_MB * CAP
    vector = pl.BlockSpec(memory_space=pltpu.VMEM)
    return pl.pallas_call(
        own_kernel,
        in_specs=[pl.BlockSpec(memory_space=pltpu.SMEM), vector],
        out_specs=[vector] * len(RETURNS),
        out_shape=[
            jax.ShapeDtypeStruct((2 * rows, group * len(offsets)), jnp.bfloat16)
            for offsets in RETURNS
        ],
        name="own_picks",
    )(z, ids)


def expert_kernel(row_ref, wgu_ref, wgu_t_ref, wd_t_ref, act_ref, *out_refs):
    width = wgu_ref.shape[0]
    hid = wd_t_ref.shape[1]
    count = row_ref.shape[0]
    pre = jnp.dot(row_ref[:, :width], wgu_ref[...], preferred_element_type=jnp.float32)
    hidden_grad = jnp.dot(row_ref[:, width:], wd_t_ref[...], preferred_element_type=jnp.float32)
    gate_pre, up_pre = pre[:, :hid], pre[:, hid:]
    sig = jax.nn.sigmoid(gate_pre)
    active = gate_pre * sig
    hidden = (active * up_pre).astype(jnp.bfloat16)
    gate_grad = hidden_grad * up_pre * sig * (1.0 + gate_pre * (1.0 - sig))
    weight = jnp.sum(hidden.astype(jnp.float32) * hidden_grad, axis=1, keepdims=True)
    weight = jnp.broadcast_to(weight, (count, LANES))
    coarse = weight.astype(jnp.bfloat16)
    fine = (weight - coarse.astype(jnp.float32)).astype(jnp.bfloat16)
    lane = lax.broadcasted_iota(jnp.int32, weight.shape, 1)
    both = jnp.concatenate(
        [gate_grad.astype(jnp.bfloat16), (hidden_grad * active).astype(jnp.bfloat16)], axis=1
    )
    act_ref[:, :hid] = hidden
    act_ref[:, hid:] = both
    marks = jnp.where(lane == 0, coarse, fine)
    sources = len(out_refs)
    size = count // sources
    group = size // EXPERTS_PLANE
    for place in range(sources):
        if sources > 1:
            out_row = lax.broadcasted_iota(jnp.int32, (size, count), 0)
            in_row = lax.broadcasted_iota(jnp.int32, (size, count), 1)
            wanted = out_row // group * (group * sources) + place * group + out_row % group
            picked = (in_row == wanted).astype(jnp.bfloat16)
            mine = jnp.dot(picked, both, preferred_element_type=jnp.float32).astype(jnp.bfloat16)
            mark = jnp.dot(picked, marks, preferred_element_type=jnp.float32).astype(jnp.bfloat16)
        else:
            mine, mark = both, marks
        out_refs[place][:, :width] = jnp.dot(
            mine, wgu_t_ref[...], preferred_element_type=jnp.float32
        ).astype(jnp.bfloat16)
        out_refs[place][:, width:] = mark


def expert_pass(rows, sources, cost, wgu, wgu_t, wd_t):
    count = rows.shape[0]
    width, pair = wgu.shape
    hid = wd_t.shape[1]
    back = jax.ShapeDtypeStruct((count // sources, width + LANES), jnp.bfloat16)
    act, *backs = pl.pallas_call(
        expert_kernel,
        out_shape=[jax.ShapeDtypeStruct((count, hid + pair), jnp.bfloat16)] + [back] * sources,
        compiler_params=pltpu.CompilerParams(vmem_limit_bytes=VMEM_LIMIT),
        cost_estimate=pl.CostEstimate(
            flops=cost, bytes_accessed=4 * wgu.size, transcendentals=0
        ),
        name="expert_rows",
    )(rows, wgu, wgu_t, wd_t)
    return act, backs


def exchanged(array, groups=None):
    return lax.all_to_all(
        array, "expert", split_axis=0, concat_axis=0, tiled=True, axis_index_groups=groups
    )


def along_z(array, by):
    size = PLANES * EXPERTS_PLANE
    step = by * EXPERTS_PLANE
    return lax.ppermute(array, "expert", [(i, (i + step) % size) for i in range(size)])


def summed_over_dp(part, dim):
    half = part.shape[dim] // 2
    me = lax.axis_index("dp")
    mine = lax.dynamic_slice_in_dim(part, me * half, half, dim)
    other = lax.dynamic_slice_in_dim(part, (1 - me) * half, half, dim)
    came = lax.ppermute(other, "dp", [(0, 1), (1, 0)])
    return (mine.astype(jnp.float32) + came.astype(jnp.float32)).astype(jnp.bfloat16)


def side_by_side(arrays):
    group = arrays[0].shape[0] // EXPERTS_PLANE
    return jnp.concatenate(
        [array.reshape(EXPERTS_PLANE, group, array.shape[1]) for array in arrays], axis=1
    )


def body(tokens, expert_ids, combine, upstream, w_gate, w_up, w_down):
    sections = lax.axis_size("section")
    tokens, upstream, ids, comb = tokens[0], upstream[0], expert_ids[0], combine[0]
    rows, width = tokens.shape
    group = rows // TOK_MB * CAP
    back_by_one = [(i, (i - 1) % sections) for i in range(sections)]
    z = (lax.axis_index("expert") // EXPERTS_PLANE).astype(jnp.int32).reshape(1)
    tie = lax.optimization_barrier

    marks = jnp.concatenate([ids.astype(jnp.bfloat16), comb], axis=1)
    raw = jnp.concatenate([tokens, upstream, jnp.pad(marks, ((0, 0), (0, LANES - 4)))], axis=1)
    from_m1, from_p1 = along_z(raw, 1), along_z(raw, -1)

    def rows_for(sources):
        send = plane_rows(z, sources)
        return send.reshape(EXPERTS_PLANE, group * len(sources), 2 * width)

    def in_plane(send, before):
        send, before = tie((send, before))
        return exchanged(send, IN_PLANE), before

    came = [exchanged(rows_for([raw]), IN_PLANE)]
    picks = own_picks(z, ids)
    gate_full = lax.all_gather(w_gate[0, 0], "dp", axis=0, tiled=True)
    up_full = lax.all_gather(w_up[0, 0], "dp", axis=0, tiled=True)
    down_full = lax.all_gather(w_down[0, 0], "dp", axis=1, tiled=True)
    wgu = jnp.concatenate([gate_full, up_full], axis=1)
    weights = (wgu, wgu.T, down_full.T)
    hid = w_gate.shape[3]
    act, back = expert_pass(came[0].reshape(-1, 2 * width), 1, COST, *weights)
    acts, backs = [act] + [None] * 4, [None] * 5
    back_0 = exchanged(back[0].reshape(EXPERTS_PLANE, group, width + LANES), IN_PLANE)
    from_p1, from_m1, weights, picks, acts[0] = tie((from_p1, from_m1, weights, picks, acts[0]))

    from_m2, from_p2 = along_z(from_m1, 1), along_z(from_p1, -1)

    def expert(turn, cost=1):
        return expert_pass(
            came[turn].reshape(-1, 2 * width),
            len(CHUNKS[turn]),
            cost,
            *weights,
        )

    got, back_0 = in_plane(rows_for([from_p1, from_m1]), back_0)
    came.append(got)

    near_a, near_b, far_a, far_b = onward_rows(z, from_m2, from_p2)
    from_m3, from_p3 = along_z(near_a, 1), along_z(near_b, -1)
    four_a = along_z(along_z(far_a, 1), 1)
    four_b = along_z(along_z(far_b, -1), -1)
    from_p2, from_m2, near_a = tie((from_p2, from_m2, near_a))
    send, came[1] = tie((rows_for([from_p2, from_m2]), came[1]))
    came.append(exchanged(send, IN_PLANE))

    acts[1], backs[1] = expert(1)
    send = side_by_side([from_p3, from_m3])
    got, came[2] = in_plane(send, came[2])
    came.append(got)

    first = [along_z(backs[1][i], by) for i, by in enumerate(CHUNKS[1])]
    came[2], first = tie((came[2], first))
    acts[2], backs[2] = expert(2, COST)
    four_a, four_b, backs[1], backs[2] = tie((four_a, four_b, backs[1], backs[2]))
    send = jnp.concatenate([four_a, four_b], axis=1).reshape(EXPERTS_PLANE, group, 2 * width)
    got, came[3] = in_plane(send, came[3])
    came.append(got)
    acts[3], backs[3] = expert(3, COST)

    first += [along_z(backs[2][i], by) for i, by in enumerate(CHUNKS[2])]
    second = [along_z(backs[3][i], by) for i, by in enumerate(CHUNKS[3])]
    first, acts[3] = tie((first, acts[3]))
    came[4], _ = tie((came[4], first))
    acts[4], backs[4] = expert(4)
    second.append(along_z(backs[4][0], CHUNKS[4][0]))
    send = side_by_side(first)
    send, came, acts = tie((send, came, acts))
    back_a = exchanged(send, IN_PLANE)
    back_b, back_a = in_plane(side_by_side(second), back_a)

    back_0, back_a, back_b = (
        array.reshape(-1, array.shape[2]) for array in (back_0, back_a, back_b)
    )
    boths = [pick[:rows] + pick[rows:] for pick in picks]

    def product(left, right):
        return jnp.dot(left, right, preferred_element_type=jnp.float32)

    grad = product(boths[0], back_0[:, :width]) + product(boths[1], back_a[:, :width])
    grad = (grad + product(boths[2], back_b[:, :width])).astype(jnp.bfloat16)
    grad = lax.ppermute(grad, "section", back_by_one)
    weight = product(picks[0], back_0[:, width:]) + product(picks[1], back_a[:, width:])
    weight = weight + product(picks[2], back_b[:, width:])
    weight = weight[:, 0] + weight[:, 1]
    weight = jnp.stack([weight[:rows], weight[rows:]], axis=1)
    grad_combine = (weight / comb.astype(jnp.float32)).astype(jnp.bfloat16)

    part_gu, part_down = 0.0, 0.0
    for row, act in zip(came, acts):
        row = row.reshape(-1, 2 * width)
        part_gu = part_gu + contract_rows(row[:, :width], act[:, hid:])
        part_down = part_down + contract_rows(act[:, :hid], row[:, width:])
    grad_gu = summed_over_dp(part_gu.astype(jnp.bfloat16), 0)
    grad_down = summed_over_dp(part_down.astype(jnp.bfloat16), 1)
    return (
        grad[None],
        grad_combine[None],
        grad_gu[:, :hid][None, None],
        grad_gu[:, hid:][None, None],
        grad_down[None, None],
    )


def solution(mesh):
    return jax.shard_map(
        body,
        mesh=mesh,
        in_specs=(
            P("section", ("expert", "dp"), None),
            P("section", ("expert", "dp"), None),
            P("section", ("expert", "dp"), None),
            P("section", ("expert", "dp"), None),
            P("section", "expert", "dp", None),
            P("section", "expert", "dp", None),
            P("section", "expert", None, "dp"),
        ),
        out_specs=(
            P("section", ("expert", "dp"), None),
            P("section", ("expert", "dp"), None),
            P("section", "expert", "dp", None),
            P("section", "expert", "dp", None),
            P("section", "expert", None, "dp"),
        ),
        check_vma=False,
    )
```

```python
import functools

import jax
import jax.numpy as jnp
from jax import lax
from jax.experimental import pallas as pl
from jax.experimental.pallas import tpu as pltpu
from jax.sharding import PartitionSpec as P

TOK_MB = 64
CAP = 4
LANES = 128
PLANES = 8
EXPERTS_PLANE = 8
IN_PLANE = [[z * EXPERTS_PLANE + c for c in range(EXPERTS_PLANE)] for z in range(PLANES)]
CHUNKS = ((0,), (1, -1), (2, -2), (3, -3), (4,))
RETURNS = ((0,), (1, -1, 2, -2), (3, -3, 4))
VMEM_LIMIT = 48 * 1024 * 1024
COST = 60000000000


def contract_rows(former, latter):
    return lax.dot_general(
        former, latter, (((0,), (0,)), ((), ())), preferred_element_type=jnp.float32
    )


def plane_tables(meta, plane, source_count, position):
    columns = EXPERTS_PLANE
    meta = meta.astype(jnp.float32).T
    rows = meta.shape[1]
    first, second = meta[0:1, :].astype(jnp.int32), meta[1:2, :].astype(jnp.int32)
    label = lax.broadcasted_iota(jnp.int32, (columns, rows), 0) + plane * columns
    hit0 = (first == label).astype(jnp.float32)
    hit1 = (second == label).astype(jnp.float32)
    row = lax.broadcasted_iota(jnp.int32, (rows, rows), 0)
    col = lax.broadcasted_iota(jnp.int32, (rows, rows), 1)
    before = ((row < col) & (row // TOK_MB == col // TOK_MB)).astype(jnp.bfloat16)
    earlier = jnp.dot(
        (hit0 + hit1).astype(jnp.bfloat16), before, preferred_element_type=jnp.float32
    )
    per_expert = rows // TOK_MB * CAP
    spot = lax.broadcasted_iota(jnp.int32, (1, rows), 1) // TOK_MB * CAP + position * per_expert
    total = columns * per_expert * source_count
    slot = lax.broadcasted_iota(jnp.int32, (total, rows), 0)

    def table(chosen, hit):
        place = jnp.sum(earlier * hit, axis=0, keepdims=True).astype(jnp.int32)
        column = chosen - plane * columns
        inside = (column >= 0) & (column < columns)
        target = jnp.where(inside, column * (per_expert * source_count) + spot + place, -1)
        return (slot == target).astype(jnp.float32)

    table0, table1 = table(first, hit0), table(second, hit1)
    plain = (table0 + table1).astype(jnp.bfloat16)
    scaled = (table0 * meta[2:3, :] + table1 * meta[3:4, :]).astype(jnp.bfloat16)
    return plain, scaled


def plane_kernel(count, x_steps, z_ref, *refs):
    mark_refs, row_refs = refs[:count], refs[count : 2 * count]
    out_ref, table = refs[2 * count :]
    step = pl.program_id(0)

    @pl.when(step == 0)
    def _():
        for place in range(count):
            plain, scaled = plane_tables(mark_refs[place][...], z_ref[0], count, place)
            table[2 * place] = plain
            table[2 * place + 1] = scaled

    kind = (step >= x_steps).astype(jnp.int32)
    total = None
    for place in range(count):
        part = jnp.dot(
            table[2 * place + kind], row_refs[place][...], preferred_element_type=jnp.float32
        )
        total = part if total is None else total + part
    out_ref[...] = total.astype(jnp.bfloat16)


def plane_rows(z, sources):
    rows, full = sources[0].shape
    count = len(sources)
    width = (full - LANES) // 2
    total = EXPERTS_PLANE * rows // TOK_MB * CAP * count
    tile = width // 2
    steps = width // tile
    return pl.pallas_call(
        functools.partial(plane_kernel, count, steps),
        grid=(2 * steps,),
        in_specs=[pl.BlockSpec(memory_space=pltpu.SMEM)]
        + [pl.BlockSpec((rows, LANES), lambda i: (0, 2 * width // LANES))] * count
        + [pl.BlockSpec((rows, tile), lambda i: (0, i))] * count,
        out_specs=pl.BlockSpec((total, tile), lambda i: (0, i)),
        out_shape=jax.ShapeDtypeStruct((total, 2 * width), jnp.bfloat16),
        scratch_shapes=[pltpu.VMEM((2 * count, total, rows), jnp.bfloat16)],
        compiler_params=pltpu.CompilerParams(vmem_limit_bytes=VMEM_LIMIT),
        name="plane_rows",
    )(z, *sources, *sources)


def onward_kernel(steps, z_ref, mark_a, mark_b, row_a, row_b, near_a, near_b, far_a, far_b, table):
    step = pl.program_id(0)
    slots = near_a.shape[0]

    @pl.when(step == 0)
    def _():
        for way, (mark_ref, sign) in enumerate(((mark_a, 1), (mark_b, -1))):
            for hop in (0, 1):
                plane = lax.rem(z_ref[0] + (PLANES + (hop + 1) * sign), PLANES)
                plain, scaled = plane_tables(mark_ref[...], plane, 1, 0)
                table[2 * way, hop * slots : (hop + 1) * slots, :] = plain
                table[2 * way + 1, hop * slots : (hop + 1) * slots, :] = scaled

    def product(table, side):
        return jnp.dot(table, side[...], preferred_element_type=jnp.float32).astype(jnp.bfloat16)

    @pl.when(step < steps)
    def _():
        both = product(table[0], row_a)
        near_a[...] = both[:slots]
        far_a[...] = both[slots:]
        near_b[...] = product(table[2, :slots, :], row_b)

    @pl.when(step >= steps)
    def _():
        near_a[...] = product(table[1, :slots, :], row_a)
        both = product(table[3], row_b)
        near_b[...] = both[:slots]
        far_b[...] = both[slots:]


def onward_rows(z, source_a, source_b):
    rows, full = source_a.shape
    width = (full - LANES) // 2
    total = EXPERTS_PLANE * rows // TOK_MB * CAP
    tile = width // 2
    steps = width // tile
    marks = pl.BlockSpec((rows, LANES), lambda i: (0, 2 * width // LANES))
    block = pl.BlockSpec((rows, tile), lambda i: (0, i))
    return pl.pallas_call(
        functools.partial(onward_kernel, steps),
        grid=(2 * steps,),
        in_specs=[pl.BlockSpec(memory_space=pltpu.SMEM), marks, marks, block, block],
        out_specs=[
            pl.BlockSpec((total, tile), lambda i: (0, i)),
            pl.BlockSpec((total, tile), lambda i: (0, i)),
            pl.BlockSpec((total, tile), lambda i: (0, jnp.minimum(i, steps - 1))),
            pl.BlockSpec((total, tile), lambda i: (0, jnp.maximum(i - steps, 0))),
        ],
        out_shape=[jax.ShapeDtypeStruct((total, 2 * width), jnp.bfloat16)] * 2
        + [jax.ShapeDtypeStruct((total, width), jnp.bfloat16)] * 2,
        scratch_shapes=[pltpu.VMEM((4, 2 * total, rows), jnp.bfloat16)],
        compiler_params=pltpu.CompilerParams(vmem_limit_bytes=VMEM_LIMIT),
        name="onward_rows",
    )(z, source_a, source_b, source_a, source_b)


def own_kernel(z_ref, ids_ref, *pick_refs):
    rows = ids_ref.shape[0]
    per_expert = rows // TOK_MB * CAP
    ids = ids_ref[...]
    label = lax.broadcasted_iota(jnp.int32, (rows, LANES), 1)
    hits = [(ids[:, k : k + 1] == label).astype(jnp.float32) for k in (0, 1)]
    row = lax.broadcasted_iota(jnp.int32, (rows, rows), 0)
    col = lax.broadcasted_iota(jnp.int32, (rows, rows), 1)
    before = ((col < row) & (col // TOK_MB == row // TOK_MB)).astype(jnp.bfloat16)
    earlier = jnp.dot(
        before, (hits[0] + hits[1]).astype(jnp.bfloat16), preferred_element_type=jnp.float32
    )
    block = lax.broadcasted_iota(jnp.int32, (rows, 1), 0) // TOK_MB
    for k in (0, 1):
        chosen = ids[:, k : k + 1]
        place = jnp.sum(earlier * hits[k], axis=1, keepdims=True).astype(jnp.int32)
        behind = (z_ref[0] - chosen // EXPERTS_PLANE + PLANES) % PLANES
        column = chosen % EXPERTS_PLANE
        for pick_ref, offsets in zip(pick_refs, RETURNS):
            spot = jnp.full((rows, 1), -1, jnp.int32)
            for turn, offset in enumerate(offsets):
                target = (column * len(offsets) + turn) * per_expert + block * CAP + place
                spot = jnp.where(behind == offset % PLANES, target, spot)
            slot = lax.broadcasted_iota(jnp.int32, (rows, pick_ref.shape[1]), 1)
            pick_ref[k * rows : (k + 1) * rows, :] = (slot == spot).astype(jnp.bfloat16)


def own_picks(z, ids):
    rows = ids.shape[0]
    group = EXPERTS_PLANE * rows // TOK_MB * CAP
    vector = pl.BlockSpec(memory_space=pltpu.VMEM)
    return pl.pallas_call(
        own_kernel,
        in_specs=[pl.BlockSpec(memory_space=pltpu.SMEM), vector],
        out_specs=[vector] * len(RETURNS),
        out_shape=[
            jax.ShapeDtypeStruct((2 * rows, group * len(offsets)), jnp.bfloat16)
            for offsets in RETURNS
        ],
        name="own_picks",
    )(z, ids)


def expert_kernel(row_ref, wgu_ref, wgu_t_ref, wd_t_ref, act_ref, *out_refs):
    width = wgu_ref.shape[0]
    hid = wd_t_ref.shape[1]
    count = row_ref.shape[0]
    pre = jnp.dot(row_ref[:, :width], wgu_ref[...], preferred_element_type=jnp.float32)
    hidden_grad = jnp.dot(row_ref[:, width:], wd_t_ref[...], preferred_element_type=jnp.float32)
    gate_pre, up_pre = pre[:, :hid], pre[:, hid:]
    sig = jax.nn.sigmoid(gate_pre)
    active = gate_pre * sig
    hidden = (active * up_pre).astype(jnp.bfloat16)
    gate_grad = hidden_grad * up_pre * sig * (1.0 + gate_pre * (1.0 - sig))
    weight = jnp.sum(hidden.astype(jnp.float32) * hidden_grad, axis=1, keepdims=True)
    weight = jnp.broadcast_to(weight, (count, LANES))
    coarse = weight.astype(jnp.bfloat16)
    fine = (weight - coarse.astype(jnp.float32)).astype(jnp.bfloat16)
    lane = lax.broadcasted_iota(jnp.int32, weight.shape, 1)
    both = jnp.concatenate(
        [gate_grad.astype(jnp.bfloat16), (hidden_grad * active).astype(jnp.bfloat16)], axis=1
    )
    act_ref[:, :hid] = hidden
    act_ref[:, hid:] = both
    marks = jnp.where(lane == 0, coarse, fine)
    sources = len(out_refs)
    size = count // sources
    group = size // EXPERTS_PLANE
    for place in range(sources):
        if sources > 1:
            out_row = lax.broadcasted_iota(jnp.int32, (size, count), 0)
            in_row = lax.broadcasted_iota(jnp.int32, (size, count), 1)
            wanted = out_row // group * (group * sources) + place * group + out_row % group
            picked = (in_row == wanted).astype(jnp.bfloat16)
            mine = jnp.dot(picked, both, preferred_element_type=jnp.float32).astype(jnp.bfloat16)
            mark = jnp.dot(picked, marks, preferred_element_type=jnp.float32).astype(jnp.bfloat16)
        else:
            mine, mark = both, marks
        out_refs[place][:, :width] = jnp.dot(
            mine, wgu_t_ref[...], preferred_element_type=jnp.float32
        ).astype(jnp.bfloat16)
        out_refs[place][:, width:] = mark


def expert_pass(rows, sources, cost, wgu, wgu_t, wd_t):
    count = rows.shape[0]
    width, pair = wgu.shape
    hid = wd_t.shape[1]
    back = jax.ShapeDtypeStruct((count // sources, width + LANES), jnp.bfloat16)
    act, *backs = pl.pallas_call(
        expert_kernel,
        out_shape=[jax.ShapeDtypeStruct((count, hid + pair), jnp.bfloat16)] + [back] * sources,
        compiler_params=pltpu.CompilerParams(vmem_limit_bytes=VMEM_LIMIT),
        cost_estimate=pl.CostEstimate(
            flops=cost, bytes_accessed=4 * wgu.size, transcendentals=0
        ),
        name="expert_rows",
    )(rows, wgu, wgu_t, wd_t)
    return act, backs


def exchanged(array, groups=None):
    return lax.all_to_all(
        array, "expert", split_axis=0, concat_axis=0, tiled=True, axis_index_groups=groups
    )


def along_z(array, by):
    size = PLANES * EXPERTS_PLANE
    step = by * EXPERTS_PLANE
    return lax.ppermute(array, "expert", [(i, (i + step) % size) for i in range(size)])


def summed_over_dp(part, dim):
    half = part.shape[dim] // 2
    me = lax.axis_index("dp")
    mine = lax.dynamic_slice_in_dim(part, me * half, half, dim)
    other = lax.dynamic_slice_in_dim(part, (1 - me) * half, half, dim)
    came = lax.ppermute(other, "dp", [(0, 1), (1, 0)])
    return (mine.astype(jnp.float32) + came.astype(jnp.float32)).astype(jnp.bfloat16)


def side_by_side(arrays):
    group = arrays[0].shape[0] // EXPERTS_PLANE
    return jnp.concatenate(
        [array.reshape(EXPERTS_PLANE, group, array.shape[1]) for array in arrays], axis=1
    )


def body(tokens, expert_ids, combine, upstream, w_gate, w_up, w_down):
    sections = lax.axis_size("section")
    tokens, upstream, ids, comb = tokens[0], upstream[0], expert_ids[0], combine[0]
    rows, width = tokens.shape
    group = rows // TOK_MB * CAP
    back_by_one = [(i, (i - 1) % sections) for i in range(sections)]
    z = (lax.axis_index("expert") // EXPERTS_PLANE).astype(jnp.int32).reshape(1)
    tie = lax.optimization_barrier

    marks = jnp.concatenate([ids.astype(jnp.bfloat16), comb], axis=1)
    raw = jnp.concatenate([tokens, upstream, jnp.pad(marks, ((0, 0), (0, LANES - 4)))], axis=1)
    from_m1, from_p1 = along_z(raw, 1), along_z(raw, -1)

    def rows_for(sources):
        send = plane_rows(z, sources)
        return send.reshape(EXPERTS_PLANE, group * len(sources), 2 * width)

    def in_plane(send, before):
        send, before = tie((send, before))
        return exchanged(send, IN_PLANE), before

    came = [exchanged(rows_for([raw]), IN_PLANE)]
    gate_full = lax.all_gather(w_gate[0, 0], "dp", axis=0, tiled=True)
    up_full = lax.all_gather(w_up[0, 0], "dp", axis=0, tiled=True)
    down_full = lax.all_gather(w_down[0, 0], "dp", axis=1, tiled=True)
    wgu = jnp.concatenate([gate_full, up_full], axis=1)
    weights = (wgu, wgu.T, down_full.T)
    hid = w_gate.shape[3]
    act, back = expert_pass(came[0].reshape(-1, 2 * width), 1, COST, *weights)
    acts, backs = [act] + [None] * 4, [None] * 5
    back_0 = exchanged(back[0].reshape(EXPERTS_PLANE, group, width + LANES), IN_PLANE)
    from_p1, from_m1, weights, acts[0], ids = tie((from_p1, from_m1, weights, acts[0], ids))

    from_m2, from_p2 = along_z(from_m1, 1), along_z(from_p1, -1)

    def expert(turn, cost=1):
        return expert_pass(
            came[turn].reshape(-1, 2 * width),
            len(CHUNKS[turn]),
            cost,
            *weights,
        )

    got, back_0 = in_plane(rows_for([from_p1, from_m1]), back_0)
    came.append(got)

    picks = own_picks(z, ids)
    from_m2, from_p2, picks = tie((from_m2, from_p2, picks))

    near_a, near_b, far_a, far_b = onward_rows(z, from_m2, from_p2)
    from_m3, from_p3 = along_z(near_a, 1), along_z(near_b, -1)
    four_a = along_z(along_z(far_a, 1), 1)
    four_b = along_z(along_z(far_b, -1), -1)
    from_p2, from_m2, near_a = tie((from_p2, from_m2, near_a))
    send, came[1] = tie((rows_for([from_p2, from_m2]), came[1]))
    came.append(exchanged(send, IN_PLANE))

    acts[1], backs[1] = expert(1)
    send = side_by_side([from_p3, from_m3])
    got, came[2] = in_plane(send, came[2])
    came.append(got)

    first = [along_z(backs[1][i], by) for i, by in enumerate(CHUNKS[1])]
    came[2], first = tie((came[2], first))
    acts[2], backs[2] = expert(2, COST)
    four_a, four_b, backs[1], backs[2] = tie((four_a, four_b, backs[1], backs[2]))
    send = jnp.concatenate([four_a, four_b], axis=1).reshape(EXPERTS_PLANE, group, 2 * width)
    got, came[3] = in_plane(send, came[3])
    came.append(got)
    acts[3], backs[3] = expert(3, COST)

    first += [along_z(backs[2][i], by) for i, by in enumerate(CHUNKS[2])]
    second = [along_z(backs[3][i], by) for i, by in enumerate(CHUNKS[3])]
    first, acts[3] = tie((first, acts[3]))
    came[4], _ = tie((came[4], first))
    acts[4], backs[4] = expert(4)
    second.append(along_z(backs[4][0], CHUNKS[4][0]))
    send = side_by_side(first)
    send, came, acts = tie((send, came, acts))
    back_a = exchanged(send, IN_PLANE)
    back_b, back_a = in_plane(side_by_side(second), back_a)

    back_0, back_a, back_b = (
        array.reshape(-1, array.shape[2]) for array in (back_0, back_a, back_b)
    )
    boths = [pick[:rows] + pick[rows:] for pick in picks]

    def product(left, right):
        return jnp.dot(left, right, preferred_element_type=jnp.float32)

    grad = product(boths[0], back_0[:, :width]) + product(boths[1], back_a[:, :width])
    grad = (grad + product(boths[2], back_b[:, :width])).astype(jnp.bfloat16)
    grad = lax.ppermute(grad, "section", back_by_one)
    weight = product(picks[0], back_0[:, width:]) + product(picks[1], back_a[:, width:])
    weight = weight + product(picks[2], back_b[:, width:])
    weight = weight[:, 0] + weight[:, 1]
    weight = jnp.stack([weight[:rows], weight[rows:]], axis=1)
    grad_combine = (weight / comb.astype(jnp.float32)).astype(jnp.bfloat16)

    part_gu, part_down = 0.0, 0.0
    for row, act in zip(came, acts):
        row = row.reshape(-1, 2 * width)
        part_gu = part_gu + contract_rows(row[:, :width], act[:, hid:])
        part_down = part_down + contract_rows(act[:, :hid], row[:, width:])
    grad_gu = summed_over_dp(part_gu.astype(jnp.bfloat16), 0)
    grad_down = summed_over_dp(part_down.astype(jnp.bfloat16), 1)
    return (
        grad[None],
        grad_combine[None],
        grad_gu[:, :hid][None, None],
        grad_gu[:, hid:][None, None],
        grad_down[None, None],
    )


def solution(mesh):
    return jax.shard_map(
        body,
        mesh=mesh,
        in_specs=(
            P("section", ("expert", "dp"), None),
            P("section", ("expert", "dp"), None),
            P("section", ("expert", "dp"), None),
            P("section", ("expert", "dp"), None),
            P("section", "expert", "dp", None),
            P("section", "expert", "dp", None),
            P("section", "expert", None, "dp"),
        ),
        out_specs=(
            P("section", ("expert", "dp"), None),
            P("section", ("expert", "dp"), None),
            P("section", "expert", "dp", None),
            P("section", "expert", "dp", None),
            P("section", "expert", None, "dp"),
        ),
        check_vma=False,
    )
```

```python
import functools

import jax
import jax.numpy as jnp
from jax import lax
from jax.experimental import pallas as pl
from jax.experimental.pallas import tpu as pltpu
from jax.sharding import PartitionSpec as P

TOK_MB = 64
CAP = 4
LANES = 128
PLANES = 8
EXPERTS_PLANE = 8
IN_PLANE = [[z * EXPERTS_PLANE + c for c in range(EXPERTS_PLANE)] for z in range(PLANES)]
CHUNKS = ((0,), (1, -1), (2, -2), (3, -3), (4,))
RETURNS = ((0,), (1, -1, 2, -2), (3, -3, 4))
VMEM_LIMIT = 48 * 1024 * 1024
COST = 60000000000


def contract_rows(former, latter):
    return lax.dot_general(
        former, latter, (((0,), (0,)), ((), ())), preferred_element_type=jnp.float32
    )


def plane_tables(meta, plane, source_count, position):
    columns = EXPERTS_PLANE
    meta = meta.astype(jnp.float32).T
    rows = meta.shape[1]
    first, second = meta[0:1, :].astype(jnp.int32), meta[1:2, :].astype(jnp.int32)
    label = lax.broadcasted_iota(jnp.int32, (columns, rows), 0) + plane * columns
    hit0 = (first == label).astype(jnp.float32)
    hit1 = (second == label).astype(jnp.float32)
    row = lax.broadcasted_iota(jnp.int32, (rows, rows), 0)
    col = lax.broadcasted_iota(jnp.int32, (rows, rows), 1)
    before = ((row < col) & (row // TOK_MB == col // TOK_MB)).astype(jnp.bfloat16)
    earlier = jnp.dot(
        (hit0 + hit1).astype(jnp.bfloat16), before, preferred_element_type=jnp.float32
    )
    per_expert = rows // TOK_MB * CAP
    spot = lax.broadcasted_iota(jnp.int32, (1, rows), 1) // TOK_MB * CAP + position * per_expert
    total = columns * per_expert * source_count
    slot = lax.broadcasted_iota(jnp.int32, (total, rows), 0)

    def table(chosen, hit):
        place = jnp.sum(earlier * hit, axis=0, keepdims=True).astype(jnp.int32)
        column = chosen - plane * columns
        inside = (column >= 0) & (column < columns)
        target = jnp.where(inside, column * (per_expert * source_count) + spot + place, -1)
        return (slot == target).astype(jnp.float32)

    table0, table1 = table(first, hit0), table(second, hit1)
    plain = (table0 + table1).astype(jnp.bfloat16)
    scaled = (table0 * meta[2:3, :] + table1 * meta[3:4, :]).astype(jnp.bfloat16)
    return plain, scaled


def plane_kernel(count, x_steps, z_ref, *refs):
    mark_refs, tok_refs, up_refs = refs[:count], refs[count : 2 * count], refs[2 * count : 3 * count]
    out_ref, table = refs[3 * count :]
    step = pl.program_id(0)

    @pl.when(step == 0)
    def _():
        for place in range(count):
            plain, scaled = plane_tables(mark_refs[place][...], z_ref[0], count, place)
            table[2 * place] = plain
            table[2 * place + 1] = scaled

    def product(kind, sides):
        total = None
        for place in range(count):
            part = jnp.dot(
                table[2 * place + kind], sides[place][...], preferred_element_type=jnp.float32
            )
            total = part if total is None else total + part
        out_ref[...] = total.astype(jnp.bfloat16)

    @pl.when(step < x_steps)
    def _():
        product(0, tok_refs)

    @pl.when(step >= x_steps)
    def _():
        product(1, up_refs)


def plane_rows(z, toks, ups):
    rows, width = ups[0].shape
    count = len(toks)
    total = EXPERTS_PLANE * rows // TOK_MB * CAP * count
    tile = width // 2
    steps = width // tile
    return pl.pallas_call(
        functools.partial(plane_kernel, count, steps),
        grid=(2 * steps,),
        in_specs=[pl.BlockSpec(memory_space=pltpu.SMEM)]
        + [pl.BlockSpec((rows, LANES), lambda i: (0, width // LANES))] * count
        + [pl.BlockSpec((rows, tile), lambda i: (0, jnp.minimum(i, steps - 1)))] * count
        + [pl.BlockSpec((rows, tile), lambda i: (0, jnp.maximum(i - steps, 0)))] * count,
        out_specs=pl.BlockSpec((total, tile), lambda i: (0, i)),
        out_shape=jax.ShapeDtypeStruct((total, 2 * width), jnp.bfloat16),
        scratch_shapes=[pltpu.VMEM((2 * count, total, rows), jnp.bfloat16)],
        compiler_params=pltpu.CompilerParams(vmem_limit_bytes=VMEM_LIMIT),
        name="plane_rows",
    )(z, *toks, *toks, *ups)


def onward_kernel(steps, z_ref, mark_a, mark_b, tok_a, tok_b, up_a, up_b, near_a, near_b, far_a, far_b, table):
    step = pl.program_id(0)
    slots = near_a.shape[0]

    @pl.when(step == 0)
    def _():
        for way, (mark_ref, sign) in enumerate(((mark_a, 1), (mark_b, -1))):
            for hop in (0, 1):
                plane = lax.rem(z_ref[0] + (PLANES + (hop + 1) * sign), PLANES)
                plain, scaled = plane_tables(mark_ref[...], plane, 1, 0)
                table[2 * way, hop * slots : (hop + 1) * slots, :] = plain
                table[2 * way + 1, hop * slots : (hop + 1) * slots, :] = scaled

    def product(table, side):
        return jnp.dot(table, side[...], preferred_element_type=jnp.float32).astype(jnp.bfloat16)

    @pl.when(step < steps)
    def _():
        both = product(table[0], tok_a)
        near_a[...] = both[:slots]
        far_a[...] = both[slots:]
        near_b[...] = product(table[2, :slots, :], tok_b)

    @pl.when(step >= steps)
    def _():
        near_a[...] = product(table[1, :slots, :], up_a)
        both = product(table[3], up_b)
        near_b[...] = both[:slots]
        far_b[...] = both[slots:]


def onward_rows(z, tok_a, tok_b, up_a, up_b):
    rows, width = up_a.shape
    total = EXPERTS_PLANE * rows // TOK_MB * CAP
    tile = width // 2
    steps = width // tile
    marks = pl.BlockSpec((rows, LANES), lambda i: (0, width // LANES))
    early = pl.BlockSpec((rows, tile), lambda i: (0, jnp.minimum(i, steps - 1)))
    late = pl.BlockSpec((rows, tile), lambda i: (0, jnp.maximum(i - steps, 0)))
    return pl.pallas_call(
        functools.partial(onward_kernel, steps),
        grid=(2 * steps,),
        in_specs=[pl.BlockSpec(memory_space=pltpu.SMEM), marks, marks, early, early, late, late],
        out_specs=[
            pl.BlockSpec((total, tile), lambda i: (0, i)),
            pl.BlockSpec((total, tile), lambda i: (0, i)),
            pl.BlockSpec((total, tile), lambda i: (0, jnp.minimum(i, steps - 1))),
            pl.BlockSpec((total, tile), lambda i: (0, jnp.maximum(i - steps, 0))),
        ],
        out_shape=[jax.ShapeDtypeStruct((total, 2 * width), jnp.bfloat16)] * 2
        + [jax.ShapeDtypeStruct((total, width), jnp.bfloat16)] * 2,
        scratch_shapes=[pltpu.VMEM((4, 2 * total, rows), jnp.bfloat16)],
        compiler_params=pltpu.CompilerParams(vmem_limit_bytes=VMEM_LIMIT),
        name="onward_rows",
    )(z, tok_a, tok_b, tok_a, tok_b, up_a, up_b)


def own_kernel(z_ref, ids_ref, *pick_refs):
    rows = ids_ref.shape[0]
    per_expert = rows // TOK_MB * CAP
    ids = ids_ref[...]
    label = lax.broadcasted_iota(jnp.int32, (rows, LANES), 1)
    hits = [(ids[:, k : k + 1] == label).astype(jnp.float32) for k in (0, 1)]
    row = lax.broadcasted_iota(jnp.int32, (rows, rows), 0)
    col = lax.broadcasted_iota(jnp.int32, (rows, rows), 1)
    before = ((col < row) & (col // TOK_MB == row // TOK_MB)).astype(jnp.bfloat16)
    earlier = jnp.dot(
        before, (hits[0] + hits[1]).astype(jnp.bfloat16), preferred_element_type=jnp.float32
    )
    block = lax.broadcasted_iota(jnp.int32, (rows, 1), 0) // TOK_MB
    for k in (0, 1):
        chosen = ids[:, k : k + 1]
        place = jnp.sum(earlier * hits[k], axis=1, keepdims=True).astype(jnp.int32)
        behind = (z_ref[0] - chosen // EXPERTS_PLANE + PLANES) % PLANES
        column = chosen % EXPERTS_PLANE
        for pick_ref, offsets in zip(pick_refs, RETURNS):
            spot = jnp.full((rows, 1), -1, jnp.int32)
            for turn, offset in enumerate(offsets):
                target = (column * len(offsets) + turn) * per_expert + block * CAP + place
                spot = jnp.where(behind == offset % PLANES, target, spot)
            slot = lax.broadcasted_iota(jnp.int32, (rows, pick_ref.shape[1]), 1)
            pick_ref[k * rows : (k + 1) * rows, :] = (slot == spot).astype(jnp.bfloat16)


def own_picks(z, ids):
    rows = ids.shape[0]
    group = EXPERTS_PLANE * rows // TOK_MB * CAP
    vector = pl.BlockSpec(memory_space=pltpu.VMEM)
    return pl.pallas_call(
        own_kernel,
        in_specs=[pl.BlockSpec(memory_space=pltpu.SMEM), vector],
        out_specs=[vector] * len(RETURNS),
        out_shape=[
            jax.ShapeDtypeStruct((2 * rows, group * len(offsets)), jnp.bfloat16)
            for offsets in RETURNS
        ],
        cost_estimate=pl.CostEstimate(flops=COST, bytes_accessed=1 << 17, transcendentals=0),
        name="own_picks",
    )(z, ids)


def expert_kernel(row_ref, wgu_ref, wgu_t_ref, wd_t_ref, act_ref, *out_refs):
    width = wgu_ref.shape[0]
    hid = wd_t_ref.shape[1]
    count = row_ref.shape[0]
    pre = jnp.dot(row_ref[:, :width], wgu_ref[...], preferred_element_type=jnp.float32)
    hidden_grad = jnp.dot(row_ref[:, width:], wd_t_ref[...], preferred_element_type=jnp.float32)
    gate_pre, up_pre = pre[:, :hid], pre[:, hid:]
    sig = jax.nn.sigmoid(gate_pre)
    active = gate_pre * sig
    hidden = (active * up_pre).astype(jnp.bfloat16)
    gate_grad = hidden_grad * up_pre * sig * (1.0 + gate_pre * (1.0 - sig))
    weight = jnp.sum(hidden.astype(jnp.float32) * hidden_grad, axis=1, keepdims=True)
    weight = jnp.broadcast_to(weight, (count, LANES))
    coarse = weight.astype(jnp.bfloat16)
    fine = (weight - coarse.astype(jnp.float32)).astype(jnp.bfloat16)
    lane = lax.broadcasted_iota(jnp.int32, weight.shape, 1)
    both = jnp.concatenate(
        [gate_grad.astype(jnp.bfloat16), (hidden_grad * active).astype(jnp.bfloat16)], axis=1
    )
    act_ref[:, :hid] = hidden
    act_ref[:, hid:] = both
    marks = jnp.where(lane == 0, coarse, fine)
    sources = len(out_refs)
    size = count // sources
    group = size // EXPERTS_PLANE
    for place in range(sources):
        if sources > 1:
            out_row = lax.broadcasted_iota(jnp.int32, (size, count), 0)
            in_row = lax.broadcasted_iota(jnp.int32, (size, count), 1)
            wanted = out_row // group * (group * sources) + place * group + out_row % group
            picked = (in_row == wanted).astype(jnp.bfloat16)
            mine = jnp.dot(picked, both, preferred_element_type=jnp.float32).astype(jnp.bfloat16)
            mark = jnp.dot(picked, marks, preferred_element_type=jnp.float32).astype(jnp.bfloat16)
        else:
            mine, mark = both, marks
        out_refs[place][:, :width] = jnp.dot(
            mine, wgu_t_ref[...], preferred_element_type=jnp.float32
        ).astype(jnp.bfloat16)
        out_refs[place][:, width:] = mark


def expert_pass(rows, sources, cost, wgu, wgu_t, wd_t):
    count = rows.shape[0]
    width, pair = wgu.shape
    hid = wd_t.shape[1]
    back = jax.ShapeDtypeStruct((count // sources, width + LANES), jnp.bfloat16)
    act, *backs = pl.pallas_call(
        expert_kernel,
        out_shape=[jax.ShapeDtypeStruct((count, hid + pair), jnp.bfloat16)] + [back] * sources,
        compiler_params=pltpu.CompilerParams(vmem_limit_bytes=VMEM_LIMIT),
        cost_estimate=pl.CostEstimate(
            flops=cost, bytes_accessed=4 * wgu.size, transcendentals=0
        ),
        name="expert_rows",
    )(rows, wgu, wgu_t, wd_t)
    return act, backs


def exchanged(array, groups=None):
    return lax.all_to_all(
        array, "expert", split_axis=0, concat_axis=0, tiled=True, axis_index_groups=groups
    )


def along_z(array, by):
    size = PLANES * EXPERTS_PLANE
    step = by * EXPERTS_PLANE
    return lax.ppermute(array, "expert", [(i, (i + step) % size) for i in range(size)])


def summed_over_dp(part, dim):
    half = part.shape[dim] // 2
    me = lax.axis_index("dp")
    mine = lax.dynamic_slice_in_dim(part, me * half, half, dim)
    other = lax.dynamic_slice_in_dim(part, (1 - me) * half, half, dim)
    came = lax.ppermute(other, "dp", [(0, 1), (1, 0)])
    return (mine.astype(jnp.float32) + came.astype(jnp.float32)).astype(jnp.bfloat16)


def side_by_side(arrays):
    group = arrays[0].shape[0] // EXPERTS_PLANE
    return jnp.concatenate(
        [array.reshape(EXPERTS_PLANE, group, array.shape[1]) for array in arrays], axis=1
    )


def body(tokens, expert_ids, combine, upstream, w_gate, w_up, w_down):
    sections = lax.axis_size("section")
    tokens, upstream, ids, comb = tokens[0], upstream[0], expert_ids[0], combine[0]
    rows, width = tokens.shape
    group = rows // TOK_MB * CAP
    back_by_one = [(i, (i - 1) % sections) for i in range(sections)]
    z = (lax.axis_index("expert") // EXPERTS_PLANE).astype(jnp.int32).reshape(1)
    tie = lax.optimization_barrier

    up_m1, up_p1 = along_z(upstream, 1), along_z(upstream, -1)
    marks = jnp.concatenate([ids.astype(jnp.bfloat16), comb], axis=1)
    marked = jnp.concatenate([tokens, jnp.pad(marks, ((0, 0), (0, LANES - 4)))], axis=1)
    tok_m1, tok_p1 = along_z(marked, 1), along_z(marked, -1)

    def rows_for(toks, ups):
        send = plane_rows(z, toks, ups)
        return send.reshape(EXPERTS_PLANE, group * len(toks), 2 * width)

    def in_plane(send, before):
        send, before = tie((send, before))
        return exchanged(send, IN_PLANE), before

    came = [exchanged(rows_for([marked], [upstream]), IN_PLANE)]
    gate_full = lax.all_gather(w_gate[0, 0], "dp", axis=0, tiled=True)
    up_full = lax.all_gather(w_up[0, 0], "dp", axis=0, tiled=True)
    down_full = lax.all_gather(w_down[0, 0], "dp", axis=1, tiled=True)
    wgu = jnp.concatenate([gate_full, up_full], axis=1)
    weights = (wgu, wgu.T, down_full.T)
    hid = w_gate.shape[3]
    act, back = expert_pass(came[0].reshape(-1, 2 * width), 1, COST, *weights)
    acts, backs = [act] + [None] * 4, [None] * 5
    back_0 = exchanged(back[0].reshape(EXPERTS_PLANE, group, width + LANES), IN_PLANE)
    tok_p1, tok_m1, weights, acts[0], ids = tie((tok_p1, tok_m1, weights, acts[0], ids))

    up_m2, up_p2 = along_z(up_m1, 1), along_z(up_p1, -1)
    tok_m2, tok_p2 = along_z(tok_m1, 1), along_z(tok_p1, -1)

    def expert(turn, cost=1):
        return expert_pass(
            came[turn].reshape(-1, 2 * width),
            len(CHUNKS[turn]),
            cost,
            *weights,
        )

    tok_p1, tok_m1, _ = tie((tok_p1, tok_m1, (up_m2, up_p2)))
    got, back_0 = in_plane(rows_for([tok_p1, tok_m1], [up_p1, up_m1]), back_0)
    came.append(got)

    picks = own_picks(z, ids)
    tok_m2, tok_p2, picks = tie((tok_m2, tok_p2, picks))

    near_a, near_b, far_a, far_b = onward_rows(z, tok_m2, tok_p2, up_m2, up_p2)
    from_m3, from_p3 = along_z(near_a, 1), along_z(near_b, -1)
    three = side_by_side([from_p3, from_m3])
    far_a, far_b = along_z(far_a, 1), along_z(far_b, -1)
    tok_p2, tok_m2, near_a = tie((tok_p2, tok_m2, near_a))
    send, came[1] = tie((rows_for([tok_p2, tok_m2], [up_p2, up_m2]), came[1]))
    came.append(exchanged(send, IN_PLANE))

    acts[1], backs[1] = expert(1)
    got, came[2] = in_plane(three, came[2])
    came.append(got)

    first = [along_z(backs[1][i], by) for i, by in enumerate(CHUNKS[1])]
    acts[2], backs[2] = expert(2, COST)
    far_a, far_b, _ = tie((far_a, far_b, backs[2]))
    four_a, four_b = along_z(far_a, 1), along_z(far_b, -1)
    four_a, four_b, first = tie((four_a, four_b, first))
    send = jnp.concatenate([four_a, four_b], axis=1).reshape(EXPERTS_PLANE, group, 2 * width)
    got, came[3] = in_plane(send, came[3])
    came.append(got)
    acts[3], backs[3] = expert(3, COST)

    first += [along_z(backs[2][i], by) for i, by in enumerate(CHUNKS[2])]
    second = [along_z(backs[3][i], by) for i, by in enumerate(CHUNKS[3])]
    first, acts[3] = tie((first, acts[3]))
    came[4], _ = tie((came[4], first))
    acts[4], backs[4] = expert(4)
    second.append(along_z(backs[4][0], CHUNKS[4][0]))
    send = side_by_side(first)
    send, came, acts = tie((send, came, acts))
    back_a = exchanged(send, IN_PLANE)
    back_b, back_a = in_plane(side_by_side(second), back_a)

    back_0, back_a, back_b = (
        array.reshape(-1, array.shape[2]) for array in (back_0, back_a, back_b)
    )
    boths = [pick[:rows] + pick[rows:] for pick in picks]

    def product(left, right):
        return jnp.dot(left, right, preferred_element_type=jnp.float32)

    grad = product(boths[0], back_0[:, :width]) + product(boths[1], back_a[:, :width])
    grad = (grad + product(boths[2], back_b[:, :width])).astype(jnp.bfloat16)
    grad = lax.ppermute(grad, "section", back_by_one)
    weight = product(picks[0], back_0[:, width:]) + product(picks[1], back_a[:, width:])
    weight = weight + product(picks[2], back_b[:, width:])
    weight = weight[:, 0] + weight[:, 1]
    weight = jnp.stack([weight[:rows], weight[rows:]], axis=1)
    grad_combine = (weight / comb.astype(jnp.float32)).astype(jnp.bfloat16)

    part_gu, part_down = 0.0, 0.0
    for row, act in zip(came, acts):
        row = row.reshape(-1, 2 * width)
        part_gu = part_gu + contract_rows(row[:, :width], act[:, hid:])
        part_down = part_down + contract_rows(act[:, :hid], row[:, width:])
    grad_gu = summed_over_dp(part_gu.astype(jnp.bfloat16), 0)
    grad_down = summed_over_dp(part_down.astype(jnp.bfloat16), 1)
    return (
        grad[None],
        grad_combine[None],
        grad_gu[:, :hid][None, None],
        grad_gu[:, hid:][None, None],
        grad_down[None, None],
    )


def solution(mesh):
    return jax.shard_map(
        body,
        mesh=mesh,
        in_specs=(
            P("section", ("expert", "dp"), None),
            P("section", ("expert", "dp"), None),
            P("section", ("expert", "dp"), None),
            P("section", ("expert", "dp"), None),
            P("section", "expert", "dp", None),
            P("section", "expert", "dp", None),
            P("section", "expert", None, "dp"),
        ),
        out_specs=(
            P("section", ("expert", "dp"), None),
            P("section", ("expert", "dp"), None),
            P("section", "expert", "dp", None),
            P("section", "expert", "dp", None),
            P("section", "expert", None, "dp"),
        ),
        check_vma=False,
    )
```

```python
import functools

import jax
import jax.numpy as jnp
from jax import lax
from jax.experimental import pallas as pl
from jax.experimental.pallas import tpu as pltpu
from jax.sharding import PartitionSpec as P

TOK_MB = 64
CAP = 4
LANES = 128
PLANES = 8
EXPERTS_PLANE = 8
IN_PLANE = [[z * EXPERTS_PLANE + c for c in range(EXPERTS_PLANE)] for z in range(PLANES)]
CHUNKS = ((0,), (1, -1), (2, -2), (3, -3), (4,))
RETURNS = ((0,), (1, -1, 2, -2), (3, -3, 4))
VMEM_LIMIT = 48 * 1024 * 1024
COST = 60000000000


def contract_rows(former, latter):
    return lax.dot_general(
        former, latter, (((0,), (0,)), ((), ())), preferred_element_type=jnp.float32
    )


def plane_tables(meta, plane, source_count, position):
    columns = EXPERTS_PLANE
    meta = meta.astype(jnp.float32).T
    rows = meta.shape[1]
    first, second = meta[0:1, :].astype(jnp.int32), meta[1:2, :].astype(jnp.int32)
    label = lax.broadcasted_iota(jnp.int32, (columns, rows), 0) + plane * columns
    hit0 = (first == label).astype(jnp.float32)
    hit1 = (second == label).astype(jnp.float32)
    row = lax.broadcasted_iota(jnp.int32, (rows, rows), 0)
    col = lax.broadcasted_iota(jnp.int32, (rows, rows), 1)
    before = ((row < col) & (row // TOK_MB == col // TOK_MB)).astype(jnp.bfloat16)
    earlier = jnp.dot(
        (hit0 + hit1).astype(jnp.bfloat16), before, preferred_element_type=jnp.float32
    )
    per_expert = rows // TOK_MB * CAP
    spot = lax.broadcasted_iota(jnp.int32, (1, rows), 1) // TOK_MB * CAP + position * per_expert
    total = columns * per_expert * source_count
    slot = lax.broadcasted_iota(jnp.int32, (total, rows), 0)

    def table(chosen, hit):
        place = jnp.sum(earlier * hit, axis=0, keepdims=True).astype(jnp.int32)
        column = chosen - plane * columns
        inside = (column >= 0) & (column < columns)
        target = jnp.where(inside, column * (per_expert * source_count) + spot + place, -1)
        return (slot == target).astype(jnp.float32)

    table0, table1 = table(first, hit0), table(second, hit1)
    plain = (table0 + table1).astype(jnp.bfloat16)
    scaled = (table0 * meta[2:3, :] + table1 * meta[3:4, :]).astype(jnp.bfloat16)
    return plain, scaled


def plane_kernel(count, x_steps, z_ref, *refs):
    mark_refs, tok_refs, up_refs = refs[:count], refs[count : 2 * count], refs[2 * count : 3 * count]
    out_ref, table = refs[3 * count :]
    step = pl.program_id(0)

    @pl.when(step == 0)
    def _():
        for place in range(count):
            plain, scaled = plane_tables(mark_refs[place][...], z_ref[0], count, place)
            table[2 * place] = plain
            table[2 * place + 1] = scaled

    def product(kind, sides):
        total = None
        for place in range(count):
            part = jnp.dot(
                table[2 * place + kind], sides[place][...], preferred_element_type=jnp.float32
            )
            total = part if total is None else total + part
        out_ref[...] = total.astype(jnp.bfloat16)

    @pl.when(step < x_steps)
    def _():
        product(0, tok_refs)

    @pl.when(step >= x_steps)
    def _():
        product(1, up_refs)


def plane_rows(z, toks, ups):
    rows, width = ups[0].shape
    count = len(toks)
    total = EXPERTS_PLANE * rows // TOK_MB * CAP * count
    tile = width // 2
    steps = width // tile
    return pl.pallas_call(
        functools.partial(plane_kernel, count, steps),
        grid=(2 * steps,),
        in_specs=[pl.BlockSpec(memory_space=pltpu.SMEM)]
        + [pl.BlockSpec((rows, LANES), lambda i: (0, width // LANES))] * count
        + [pl.BlockSpec((rows, tile), lambda i: (0, jnp.minimum(i, steps - 1)))] * count
        + [pl.BlockSpec((rows, tile), lambda i: (0, jnp.maximum(i - steps, 0)))] * count,
        out_specs=pl.BlockSpec((total, tile), lambda i: (0, i)),
        out_shape=jax.ShapeDtypeStruct((total, 2 * width), jnp.bfloat16),
        scratch_shapes=[pltpu.VMEM((2 * count, total, rows), jnp.bfloat16)],
        compiler_params=pltpu.CompilerParams(vmem_limit_bytes=VMEM_LIMIT),
        name="plane_rows",
    )(z, *toks, *toks, *ups)


def onward_kernel(steps, z_ref, mark_a, mark_b, tok_a, tok_b, up_a, up_b, near_a, near_b, far_a, far_b, table):
    step = pl.program_id(0)
    slots = near_a.shape[0]

    @pl.when(step == 0)
    def _():
        for way, (mark_ref, sign) in enumerate(((mark_a, 1), (mark_b, -1))):
            for hop in (0, 1):
                plane = lax.rem(z_ref[0] + (PLANES + (hop + 1) * sign), PLANES)
                plain, scaled = plane_tables(mark_ref[...], plane, 1, 0)
                table[2 * way, hop * slots : (hop + 1) * slots, :] = plain
                table[2 * way + 1, hop * slots : (hop + 1) * slots, :] = scaled

    def product(table, side):
        return jnp.dot(table, side[...], preferred_element_type=jnp.float32).astype(jnp.bfloat16)

    @pl.when(step < steps)
    def _():
        both = product(table[0], tok_a)
        near_a[...] = both[:slots]
        far_a[...] = both[slots:]
        near_b[...] = product(table[2, :slots, :], tok_b)

    @pl.when(step >= steps)
    def _():
        near_a[...] = product(table[1, :slots, :], up_a)
        both = product(table[3], up_b)
        near_b[...] = both[:slots]
        far_b[...] = both[slots:]


def onward_rows(z, tok_a, tok_b, up_a, up_b):
    rows, width = up_a.shape
    total = EXPERTS_PLANE * rows // TOK_MB * CAP
    tile = width // 2
    steps = width // tile
    marks = pl.BlockSpec((rows, LANES), lambda i: (0, width // LANES))
    early = pl.BlockSpec((rows, tile), lambda i: (0, jnp.minimum(i, steps - 1)))
    late = pl.BlockSpec((rows, tile), lambda i: (0, jnp.maximum(i - steps, 0)))
    return pl.pallas_call(
        functools.partial(onward_kernel, steps),
        grid=(2 * steps,),
        in_specs=[pl.BlockSpec(memory_space=pltpu.SMEM), marks, marks, early, early, late, late],
        out_specs=[
            pl.BlockSpec((total, tile), lambda i: (0, i)),
            pl.BlockSpec((total, tile), lambda i: (0, i)),
            pl.BlockSpec((total, tile), lambda i: (0, jnp.minimum(i, steps - 1))),
            pl.BlockSpec((total, tile), lambda i: (0, jnp.maximum(i - steps, 0))),
        ],
        out_shape=[jax.ShapeDtypeStruct((total, 2 * width), jnp.bfloat16)] * 2
        + [jax.ShapeDtypeStruct((total, width), jnp.bfloat16)] * 2,
        scratch_shapes=[pltpu.VMEM((4, 2 * total, rows), jnp.bfloat16)],
        compiler_params=pltpu.CompilerParams(vmem_limit_bytes=VMEM_LIMIT),
        name="onward_rows",
    )(z, tok_a, tok_b, tok_a, tok_b, up_a, up_b)


def own_kernel(z_ref, ids_ref, *pick_refs):
    rows = ids_ref.shape[0]
    per_expert = rows // TOK_MB * CAP
    ids = ids_ref[...]
    label = lax.broadcasted_iota(jnp.int32, (rows, LANES), 1)
    hits = [(ids[:, k : k + 1] == label).astype(jnp.float32) for k in (0, 1)]
    row = lax.broadcasted_iota(jnp.int32, (rows, rows), 0)
    col = lax.broadcasted_iota(jnp.int32, (rows, rows), 1)
    before = ((col < row) & (col // TOK_MB == row // TOK_MB)).astype(jnp.bfloat16)
    earlier = jnp.dot(
        before, (hits[0] + hits[1]).astype(jnp.bfloat16), preferred_element_type=jnp.float32
    )
    block = lax.broadcasted_iota(jnp.int32, (rows, 1), 0) // TOK_MB
    for k in (0, 1):
        chosen = ids[:, k : k + 1]
        place = jnp.sum(earlier * hits[k], axis=1, keepdims=True).astype(jnp.int32)
        behind = (z_ref[0] - chosen // EXPERTS_PLANE + PLANES) % PLANES
        column = chosen % EXPERTS_PLANE
        for pick_ref, offsets in zip(pick_refs, RETURNS):
            spot = jnp.full((rows, 1), -1, jnp.int32)
            for turn, offset in enumerate(offsets):
                target = (column * len(offsets) + turn) * per_expert + block * CAP + place
                spot = jnp.where(behind == offset % PLANES, target, spot)
            slot = lax.broadcasted_iota(jnp.int32, (rows, pick_ref.shape[1]), 1)
            pick_ref[k * rows : (k + 1) * rows, :] = (slot == spot).astype(jnp.bfloat16)


def own_picks(z, ids):
    rows = ids.shape[0]
    group = EXPERTS_PLANE * rows // TOK_MB * CAP
    vector = pl.BlockSpec(memory_space=pltpu.VMEM)
    return pl.pallas_call(
        own_kernel,
        in_specs=[pl.BlockSpec(memory_space=pltpu.SMEM), vector],
        out_specs=[vector] * len(RETURNS),
        out_shape=[
            jax.ShapeDtypeStruct((2 * rows, group * len(offsets)), jnp.bfloat16)
            for offsets in RETURNS
        ],
        cost_estimate=pl.CostEstimate(flops=COST, bytes_accessed=1 << 17, transcendentals=0),
        name="own_picks",
    )(z, ids)


def expert_kernel(row_ref, wgu_ref, wgu_t_ref, wd_t_ref, act_ref, *out_refs):
    width = wgu_ref.shape[0]
    hid = wd_t_ref.shape[1]
    count = row_ref.shape[0]
    pre = jnp.dot(row_ref[:, :width], wgu_ref[...], preferred_element_type=jnp.float32)
    hidden_grad = jnp.dot(row_ref[:, width:], wd_t_ref[...], preferred_element_type=jnp.float32)
    gate_pre, up_pre = pre[:, :hid], pre[:, hid:]
    sig = jax.nn.sigmoid(gate_pre)
    active = gate_pre * sig
    hidden = (active * up_pre).astype(jnp.bfloat16)
    gate_grad = hidden_grad * up_pre * sig * (1.0 + gate_pre * (1.0 - sig))
    weight = jnp.sum(hidden.astype(jnp.float32) * hidden_grad, axis=1, keepdims=True)
    weight = jnp.broadcast_to(weight, (count, LANES))
    coarse = weight.astype(jnp.bfloat16)
    fine = (weight - coarse.astype(jnp.float32)).astype(jnp.bfloat16)
    lane = lax.broadcasted_iota(jnp.int32, weight.shape, 1)
    both = jnp.concatenate(
        [gate_grad.astype(jnp.bfloat16), (hidden_grad * active).astype(jnp.bfloat16)], axis=1
    )
    act_ref[:, :hid] = hidden
    act_ref[:, hid:] = both
    marks = jnp.where(lane == 0, coarse, fine)
    sources = len(out_refs)
    size = count // sources
    group = size // EXPERTS_PLANE
    for place in range(sources):
        if sources > 1:
            out_row = lax.broadcasted_iota(jnp.int32, (size, count), 0)
            in_row = lax.broadcasted_iota(jnp.int32, (size, count), 1)
            wanted = out_row // group * (group * sources) + place * group + out_row % group
            picked = (in_row == wanted).astype(jnp.bfloat16)
            mine = jnp.dot(picked, both, preferred_element_type=jnp.float32).astype(jnp.bfloat16)
            mark = jnp.dot(picked, marks, preferred_element_type=jnp.float32).astype(jnp.bfloat16)
        else:
            mine, mark = both, marks
        out_refs[place][:, :width] = jnp.dot(
            mine, wgu_t_ref[...], preferred_element_type=jnp.float32
        ).astype(jnp.bfloat16)
        out_refs[place][:, width:] = mark


def expert_pass(rows, sources, cost, wgu, wgu_t, wd_t):
    count = rows.shape[0]
    width, pair = wgu.shape
    hid = wd_t.shape[1]
    back = jax.ShapeDtypeStruct((count // sources, width + LANES), jnp.bfloat16)
    act, *backs = pl.pallas_call(
        expert_kernel,
        out_shape=[jax.ShapeDtypeStruct((count, hid + pair), jnp.bfloat16)] + [back] * sources,
        compiler_params=pltpu.CompilerParams(vmem_limit_bytes=VMEM_LIMIT),
        cost_estimate=pl.CostEstimate(
            flops=cost, bytes_accessed=4 * wgu.size, transcendentals=0
        ),
        name="expert_rows",
    )(rows, wgu, wgu_t, wd_t)
    return act, backs


def exchanged(array, groups=None):
    return lax.all_to_all(
        array, "expert", split_axis=0, concat_axis=0, tiled=True, axis_index_groups=groups
    )


def along_z(array, by):
    size = PLANES * EXPERTS_PLANE
    step = by * EXPERTS_PLANE
    return lax.ppermute(array, "expert", [(i, (i + step) % size) for i in range(size)])


def summed_over_dp(part, dim):
    half = part.shape[dim] // 2
    me = lax.axis_index("dp")
    mine = lax.dynamic_slice_in_dim(part, me * half, half, dim)
    other = lax.dynamic_slice_in_dim(part, (1 - me) * half, half, dim)
    came = lax.ppermute(other, "dp", [(0, 1), (1, 0)])
    return (mine.astype(jnp.float32) + came.astype(jnp.float32)).astype(jnp.bfloat16)


def side_by_side(arrays):
    group = arrays[0].shape[0] // EXPERTS_PLANE
    return jnp.concatenate(
        [array.reshape(EXPERTS_PLANE, group, array.shape[1]) for array in arrays], axis=1
    )


def body(tokens, expert_ids, combine, upstream, w_gate, w_up, w_down):
    sections = lax.axis_size("section")
    tokens, upstream, ids, comb = tokens[0], upstream[0], expert_ids[0], combine[0]
    rows, width = tokens.shape
    group = rows // TOK_MB * CAP
    back_by_one = [(i, (i - 1) % sections) for i in range(sections)]
    z = (lax.axis_index("expert") // EXPERTS_PLANE).astype(jnp.int32).reshape(1)
    tie = lax.optimization_barrier

    up_m1, up_p1 = along_z(upstream, 1), along_z(upstream, -1)
    marks = jnp.concatenate([ids.astype(jnp.bfloat16), comb], axis=1)
    marked = jnp.concatenate([tokens, jnp.pad(marks, ((0, 0), (0, LANES - 4)))], axis=1)
    tok_m1, tok_p1 = along_z(marked, 1), along_z(marked, -1)

    def rows_for(toks, ups):
        send = plane_rows(z, toks, ups)
        return send.reshape(EXPERTS_PLANE, group * len(toks), 2 * width)

    def in_plane(send, before):
        send, before = tie((send, before))
        return exchanged(send, IN_PLANE), before

    came = [exchanged(rows_for([marked], [upstream]), IN_PLANE)]
    gate_full = lax.all_gather(w_gate[0, 0], "dp", axis=0, tiled=True)
    up_full = lax.all_gather(w_up[0, 0], "dp", axis=0, tiled=True)
    down_full = lax.all_gather(w_down[0, 0], "dp", axis=1, tiled=True)
    wgu = jnp.concatenate([gate_full, up_full], axis=1)
    weights = (wgu, wgu.T, down_full.T)
    hid = w_gate.shape[3]
    act, back = expert_pass(came[0].reshape(-1, 2 * width), 1, COST, *weights)
    acts, backs = [act] + [None] * 4, [None] * 5
    back_0 = exchanged(back[0].reshape(EXPERTS_PLANE, group, width + LANES), IN_PLANE)
    tok_p1, tok_m1, weights, acts[0], ids = tie((tok_p1, tok_m1, weights, acts[0], ids))

    up_m2, up_p2 = along_z(up_m1, 1), along_z(up_p1, -1)
    tok_m2, tok_p2 = along_z(tok_m1, 1), along_z(tok_p1, -1)

    def expert(turn, cost=1):
        return expert_pass(
            came[turn].reshape(-1, 2 * width),
            len(CHUNKS[turn]),
            cost,
            *weights,
        )

    tok_p1, tok_m1, _ = tie((tok_p1, tok_m1, (up_m2, up_p2)))
    got, back_0 = in_plane(rows_for([tok_p1, tok_m1], [up_p1, up_m1]), back_0)
    came.append(got)

    picks = own_picks(z, ids)
    tok_m2, tok_p2, picks = tie((tok_m2, tok_p2, picks))

    near_a, near_b, far_a, far_b = onward_rows(z, tok_m2, tok_p2, up_m2, up_p2)
    from_m3, from_p3 = along_z(near_a, 1), along_z(near_b, -1)
    three = side_by_side([from_p3, from_m3])
    far_a, far_b = along_z(far_a, 1), along_z(far_b, -1)
    tok_p2, tok_m2, near_a = tie((tok_p2, tok_m2, near_a))
    send, came[1] = tie((rows_for([tok_p2, tok_m2], [up_p2, up_m2]), came[1]))
    came.append(exchanged(send, IN_PLANE))

    acts[1], backs[1] = expert(1)
    got, came[2] = in_plane(three, came[2])
    came.append(got)

    first = [along_z(backs[1][i], by) for i, by in enumerate(CHUNKS[1])]
    acts[2], backs[2] = expert(2, COST)
    far_a, far_b, _ = tie((far_a, far_b, backs[2]))
    four_a, four_b = along_z(far_a, 1), along_z(far_b, -1)
    four_a, four_b, first = tie((four_a, four_b, first))
    send = jnp.concatenate([four_a, four_b], axis=1).reshape(EXPERTS_PLANE, group, 2 * width)
    got, came[3] = in_plane(send, came[3])
    came.append(got)
    acts[3], backs[3] = expert(3, COST)

    first += [along_z(backs[2][i], by) for i, by in enumerate(CHUNKS[2])]
    second = [along_z(backs[3][i], by) for i, by in enumerate(CHUNKS[3])]
    first, acts[3] = tie((first, acts[3]))
    came[4], _ = tie((came[4], first))
    acts[4], backs[4] = expert(4)
    second.append(along_z(backs[4][0], CHUNKS[4][0]))
    send = side_by_side(first)
    send, came, acts = tie((send, came, acts))
    back_a = exchanged(send, IN_PLANE)
    back_b, back_a = in_plane(side_by_side(second), back_a)

    back_0, back_a, back_b = (
        array.reshape(-1, array.shape[2]) for array in (back_0, back_a, back_b)
    )
    boths = [pick[:rows] + pick[rows:] for pick in picks]

    def product(left, right):
        return jnp.dot(left, right, preferred_element_type=jnp.float32)

    back_0, _ = tie((back_0, back_a))
    grad = product(boths[0], back_0[:, :width]) + product(boths[1], back_a[:, :width])
    grad = (grad + product(boths[2], back_b[:, :width])).astype(jnp.bfloat16)
    grad = lax.ppermute(grad, "section", back_by_one)
    weight = product(picks[0], back_0[:, width:]) + product(picks[1], back_a[:, width:])
    weight = weight + product(picks[2], back_b[:, width:])
    weight = weight[:, 0] + weight[:, 1]
    weight = jnp.stack([weight[:rows], weight[rows:]], axis=1)
    grad_combine = (weight / comb.astype(jnp.float32)).astype(jnp.bfloat16)

    part_gu, part_down = 0.0, 0.0
    for row, act in zip(came, acts):
        row = row.reshape(-1, 2 * width)
        part_gu = part_gu + contract_rows(row[:, :width], act[:, hid:])
        part_down = part_down + contract_rows(act[:, :hid], row[:, width:])
    grad_gu = summed_over_dp(part_gu.astype(jnp.bfloat16), 0)
    grad_down = summed_over_dp(part_down.astype(jnp.bfloat16), 1)
    return (
        grad[None],
        grad_combine[None],
        grad_gu[:, :hid][None, None],
        grad_gu[:, hid:][None, None],
        grad_down[None, None],
    )


def solution(mesh):
    return jax.shard_map(
        body,
        mesh=mesh,
        in_specs=(
            P("section", ("expert", "dp"), None),
            P("section", ("expert", "dp"), None),
            P("section", ("expert", "dp"), None),
            P("section", ("expert", "dp"), None),
            P("section", "expert", "dp", None),
            P("section", "expert", "dp", None),
            P("section", "expert", None, "dp"),
        ),
        out_specs=(
            P("section", ("expert", "dp"), None),
            P("section", ("expert", "dp"), None),
            P("section", "expert", "dp", None),
            P("section", "expert", "dp", None),
            P("section", "expert", None, "dp"),
        ),
        check_vma=False,
    )
```
